128 devices in a mesh: horiz: 8 (over x, y_lo), vert: 16 (over z, y_hi, core).
Axes of the slice: x: 4, y: 4 (y_hi: 2, y_lo: 2; y = y_hi * 2 + y_lo), z: 4, core: 2. Of those that a mesh axis runs over, the one named last changes fastest.
Arguments:
- air_seed: float32 [5, 256, 256, 256], P(None, 'vert', 'horiz'), may hold values from -6 to 6
- wall_seed: float32 [8, 131072], P(None, ('horiz', 'vert')), may hold values from -6 to 6
- speed: float32 [3, 256, 256, 256], P(None, 'vert', 'horiz'), may hold values from 0.01 to 0.08
- upwind: int32 [3, 256, 256, 256], P(None, 'vert', 'horiz'), may hold values 0 or 1
- diffusivity: float32 [5], replicated, may hold values from 0.01 to 0.06
- conductivity: float32 [7, 131072], P(None, ('horiz', 'vert')), may hold values from 0.02 to 0.2
- wall_saved: float32 [4, 8, 131072], P(None, None, ('horiz', 'vert')), may hold values from -6 to 6
- heat_table: float32 [8], replicated, may hold values from 0.05 to 0.4
- interface: int32 [131072], P(('horiz', 'vert')), may hold values from 0 to 131071
- owner: int32 [131072, 1], P(('horiz', 'vert')), may hold values from 0 to 15; in each aligned block of 1024 rows (0 to 1023, 1024 to 2047, ...) at most 256 rows name the same one
- material: int32 [131072], P(('horiz', 'vert')), may hold values from 0 to 7
Outputs:
- air_adjoint: float32 [5, 256, 256, 256], P(None, 'vert', 'horiz')
- wall_adjoint: float32 [8, 131072], P(None, ('horiz', 'vert'))
- conductivity_grad: float32 [7, 131072], P(None, ('horiz', 'vert'))
The draws below stay inside these ranges and needn't reach their ends.
Inputs may be any that keep to these rules, and one draw needn't show every extreme that they name: `owner`: in each aligned block of 1024 wall columns (those of one device) at most 256 columns name one vertical brick, and in every draw some brick is named by exactly 256 of them.
All inputs are finite; a program needn't handle non-finite values. No bound on the sum of `upwind` on one device may be relied on, other than what follows from the above.
Results may differ from the reference program's by a relative error of at most 0.00014.
Values sent between devices are 32-bit elements; how exact they have to be, the bound alone decides.
A program may use at most 128 MiB of HBM per device.

```python
import math
import jax
import jax.numpy as jnp
import numpy as np
from jax import lax

F = 5
L = 8
K = 4
MATS = 8
CZ = 16
CX = 32
NY = 256
W_DEV = 1024
CAP = 256
NZ = 256
NX = 256
WALLS = 131072
N_VERT = 16


def with_ends(entries, own_key, low, top_value):
    shape = entries.shape
    spot = [jax.random.randint(jax.random.fold_in(own_key, axis), (), 0, shape[axis]) for axis in range(len(shape))]
    entries = entries.at[tuple(spot)].set(low)
    longest = shape.index(max(shape))
    spot[longest] = (spot[longest] + 1) % shape[longest]
    return entries.at[tuple(spot)].set(top_value)


def level_of(own_key, extent, cuts, smallest, top_value):
    factor_of = 1.0
    for dim, parts in cuts:
        draws = jax.random.uniform(jax.random.fold_in(jax.random.fold_in(own_key, 6), dim), (parts,), jnp.float32, smallest / len(cuts), top_value / len(cuts))
        factor_of = factor_of * jnp.repeat(jnp.exp(draws), extent[dim] // parts).reshape((-1,) + (1,) * (len(extent) - 1 - dim))
    return factor_of


def assign_block(rng, own, number, rows, number_of, top, bound, slope):
    ranking = jax.random.permutation(rng, number_of)
    packed, common = portions_of(number_of, rows * top, bound, slope, True), portions_of(number_of, rows * top, bound, slope, False)
    places = jnp.arange(number_of)

    def named(lengths, turn):
        used = int((lengths > 0).sum())
        fixed = max(1, used // 4)
        shifted = fixed + (places - fixed + turn * (used - fixed)) % max(1, number_of - fixed)
        return jnp.zeros((number_of,), jnp.int32).at[ranking[jnp.where(places < fixed, places, shifted)]].set(jnp.asarray(lengths, jnp.int32))

    lengths = jnp.where(number % 4 == 0, named(packed, number // 4), named(common, number - number // 4 - 1))
    mixed = jax.random.permutation(jax.random.fold_in(own, 3), number_of)
    source_of, receiver = mixed[0:number_of // 2 * 2:2], mixed[1:number_of // 2 * 2:2]
    margin = jnp.minimum(lengths[source_of] - 1, bound - lengths[receiver]) // 2
    margin = jnp.where((source_of == ranking[0]) | (receiver == ranking[0]) | (lengths[receiver] == 0), 0, jnp.maximum(margin, 0))
    shifted = jax.random.randint(jax.random.fold_in(own, 4), (number_of // 2,), 0, 1 << 20) % (margin + 1)
    lengths = lengths.at[source_of].add(-shifted).at[receiver].add(shifted)
    items = jnp.searchsorted(jnp.cumsum(lengths), jnp.arange(rows * top), side="right").astype(jnp.int32)
    listing = items.reshape(top, rows).T
    listing = listing[jax.random.permutation(jax.random.fold_in(own, 1), rows)]
    turn = jax.random.randint(jax.random.fold_in(own, 2), (rows, 1), 0, top)
    return jnp.take_along_axis(listing, (jnp.arange(top)[None, :] + turn) % top, axis=1)


def portions_of(number_of, total, limit, skew, full):
    loads = [(1 << 20) // math.isqrt(standing ** skew) + 1 for standing in range(1, number_of + 1)]
    largest = limit if full else min(limit, max(-(-total // number_of), total * loads[0] // sum(loads)))
    least = 1 if total - largest >= number_of - 1 else 0
    counts, rest = [largest] + [least] * (number_of - 1), total - largest - least * (number_of - 1)
    while rest > 0:
        candidates = [i for i in range(1, number_of) if counts[i] < largest] or [i for i in range(1, number_of) if counts[i] < limit]
        whole, remaining = sum([loads[i] for i in candidates]), rest
        for i in candidates:
            addition = min(limit - counts[i], max(1, remaining * loads[i] // whole), rest)
            counts[i] = counts[i] + addition
            rest = rest - addition
    return np.array(counts)


def bell_draw(rng, dims, width, most, cuts=(), kind=jnp.bfloat16):
    drawn = jax.random.normal(rng, dims, jnp.float32) * width
    if len(cuts) > 0:
        drawn = level_of(rng, dims, cuts, -0.22, 0.18) * drawn
    return jnp.clip(drawn, min=-most, max=most).astype(kind)


def setup_inputs(seed: int = 0) -> dict:
    arg_keys = jax.random.split(jax.random.key(seed), 12)
    air_seed = bell_draw(arg_keys[0], (F, NZ, NX, NY), 1.0, 6.0, ((1, 16), (2, 8)), jnp.float32)
    wall_seed = bell_draw(arg_keys[1], (L, WALLS), 1.0, 6.0, ((1, 128),), jnp.float32)
    speed = jnp.clip(0.01 + 0.07 * jax.random.uniform(arg_keys[2], (3, NZ, NX, NY), jnp.float32) ** level_of(arg_keys[2], (3, NZ, NX, NY), ((1, 16), (2, 8)), -0.2, 0.2), 0.01, 0.08)
    upwind = with_ends((jax.random.randint(arg_keys[3], (3, NZ, NX, NY), 0, 2) < 1).astype(jnp.int32), jax.random.fold_in(arg_keys[3], 1), 0, 1)
    diffusivity = jnp.clip(jax.random.uniform(arg_keys[4], (F,), jnp.float32, 0.01, 0.06), 0.01, 0.06)
    conductivity = jnp.clip(jnp.exp(math.log(0.2) - 2.3025851 * jax.random.uniform(arg_keys[5], (L - 1, WALLS), jnp.float32) ** level_of(arg_keys[5], (L - 1, WALLS), ((1, 128),), -0.2, 0.2)), 0.02, 0.2)
    wall_saved = bell_draw(arg_keys[6], (K, L, WALLS), 1.0, 6.0, ((2, 128),), jnp.float32)
    heat_table = jnp.clip(jnp.exp(jax.random.uniform(arg_keys[7], (MATS,), jnp.float32, math.log(0.05), math.log(0.4))), 0.05, 0.4)
    interface = with_ends(jax.random.randint(arg_keys[8], (WALLS,), 0, CZ * CX * NY), jax.random.fold_in(arg_keys[8], 1), 0, (CZ * CX * NY) - 1).astype(jnp.int32)
    owner_keys = jax.random.split(jax.random.fold_in(arg_keys[9], 1), WALLS // W_DEV)
    owner_turns = jax.random.permutation(jax.random.fold_in(arg_keys[9], 3), WALLS // W_DEV)
    owner = jax.vmap(lambda own, number: assign_block(jax.random.fold_in(arg_keys[9], 2), own, number, W_DEV, N_VERT, 1, CAP, 2))(owner_keys, owner_turns).reshape((WALLS, 1))
    material = with_ends(jax.random.randint(arg_keys[10], (WALLS,), 0, MATS), jax.random.fold_in(arg_keys[10], 1), 0, MATS - 1).astype(jnp.int32)
    return dict(air_seed=air_seed, wall_seed=wall_seed, speed=speed, upwind=upwind, diffusivity=diffusivity, conductivity=conductivity, wall_saved=wall_saved, heat_table=heat_table, interface=interface, owner=owner, material=material)


RATIO = 0.5


def shifted_lower(field, axis):
    widths = [(0, 0)] * field.ndim
    widths[axis] = (1, 0)
    padded = jnp.pad(field, widths)
    return lax.slice_in_dim(padded, 0, field.shape[axis], axis=axis)


def air_core(padded, outflow, inflow_z, inflow_x, inflow_y, diffusivity):
    centre = padded[:, 1:-1, 1:-1, 1:-1]
    above = padded[:, 2:, 1:-1, 1:-1]
    below = padded[:, :-2, 1:-1, 1:-1]
    east = padded[:, 1:-1, 2:, 1:-1]
    west = padded[:, 1:-1, :-2, 1:-1]
    north = padded[:, 1:-1, 1:-1, 2:]
    south = padded[:, 1:-1, 1:-1, :-2]
    lapl = above + below + east + west + north + south - 6.0 * centre
    advect = outflow[0] * (above - centre) + inflow_z * (centre - below)
    advect = advect + outflow[1] * (east - centre) + inflow_x * (centre - west)
    advect = advect + outflow[2] * (north - centre) + inflow_y * (centre - south)
    return centre + diffusivity[:, None, None, None] * lapl + advect


def wall_back(wall_adj, cond):
    flux = cond * (wall_adj[1:] - wall_adj[:-1])
    upper = jnp.pad(flux, ((0, 1), (0, 0)))
    lower = jnp.pad(flux, ((1, 0), (0, 0)))
    return wall_adj + upper - lower


def reference(air_seed, wall_seed, speed, upwind, diffusivity, conductivity, wall_saved, heat_table, interface, owner, material):
    upwind_f = upwind.astype(jnp.float32)
    outflow = speed * upwind_f
    inflow = speed * (1.0 - upwind_f)
    inflow_z = shifted_lower(inflow[0], 0)
    inflow_x = shifted_lower(inflow[1], 1)
    inflow_y = shifted_lower(inflow[2], 2)
    walls = interface.shape[0]
    wall_ids = jnp.arange(walls, dtype=jnp.int32)
    hblock = (wall_ids // W_DEV) // N_VERT
    zpos = owner[:, 0] * CZ + interface // (CX * NY)
    xpos = hblock * CX + (interface // NY) % CX
    ypos = interface % NY
    face_cell = ((zpos * NX + xpos) * NY + ypos).astype(jnp.int32)
    hcoef = heat_table[material]
    air = air_seed
    wall_adj = wall_seed
    grad = jnp.zeros(conductivity.shape, jnp.float32)
    for step in reversed(range(K)):
        saved = wall_saved[step]
        grad = grad - (saved[1:] - saved[:-1]) * (wall_adj[1:] - wall_adj[:-1])
        fetched = air[0].reshape(-1)[face_cell]
        flow = hcoef * (wall_adj[0] - RATIO * fetched)
        padded = jnp.pad(air, ((0, 0), (1, 1), (1, 1), (1, 1)))
        fresh = air_core(padded, outflow, inflow_z, inflow_x, inflow_y, diffusivity)
        flat = fresh[0].reshape(-1).at[face_cell].add(flow)
        air = fresh.at[0].set(flat.reshape(fresh.shape[1:]))
        wall_adj = wall_back(wall_adj, conductivity)
        wall_adj = wall_adj.at[0].add(-flow)
    return air, wall_adj, grad
```

```python
import functools

import jax
import jax.numpy as jnp
from jax import lax
from jax.experimental import pallas as pl
from jax.experimental.pallas import tpu as pltpu
from jax.sharding import PartitionSpec as P

F32, BF16, I32 = jnp.float32, jnp.bfloat16, jnp.int32
MESH = pl.DeviceIdType.MESH
LANES, SUBS = 128, 8
RATIO = 0.5
ROWS = 8
NT = (((1,), (1,)), ((), ()))


def dot(a, b):
    return jnp.dot(a, b, preferred_element_type=F32)


def dot_nt(a, b):
    return lax.dot_general(a, b, NT, preferred_element_type=F32)


def split(value, parts):
    pieces = []
    for _ in range(parts):
        piece = value.astype(BF16).astype(F32)
        pieces.append(piece)
        value = value - piece
    return pieces


def wall_back(p, cond8):
    flux = cond8 * (pltpu.roll(p, ROWS - 1, 0) - p)
    return p + flux - pltpu.roll(flux, 1, 0)


def kernel(
    dims,
    kappa_ref,
    table_ref,
    wall_ref,
    cond_ref,
    saved_ref,
    face_ref,
    owner_ref,
    mat_ref,
    air_hbm,
    speed_hbm,
    upwind_hbm,
    air_out,
    wall_out,
    grad_out,
    air,
    speed,
    upwind,
    in_z,
    in_x,
    in_y,
    centre_c,
    out_x_last,
    in_x_last,
    in_z_halo,
    in_x_halo,
    halo_z,
    halo_x,
    edge_x,
    fix_x,
    field_hi,
    field_lo,
    row_hot,
    col_hot,
    added,
    parts_ref,
    rank_hot,
    parcel,
    served,
    result,
    returned,
    load_sem,
    store_sem,
    in_send,
    in_recv,
    halo_send,
    halo_recv,
    parcel_send,
    parcel_recv,
    return_send,
    return_recv,
):
    steps, groups, columns = dims
    fields, depth, breadth, span = air_out.shape
    walls = face_ref.shape[1]
    cap = rank_hot.shape[0]
    rows = depth * breadth
    x_tiles = breadth // SUBS
    me = lax.axis_index("vert")
    col = lax.axis_index("horiz")
    above, below = lax.rem(me + 1, groups), lax.rem(me + groups - 1, groups)
    east, west = lax.rem(col + 1, columns), lax.rem(col + columns - 1, columns)
    has_below = jnp.where(me > 0, 1.0, 0.0).astype(F32)
    has_above = jnp.where(me < groups - 1, 1.0, 0.0).astype(F32)
    has_west = jnp.where(col > 0, 1.0, 0.0).astype(F32)
    has_east = jnp.where(col < columns - 1, 1.0, 0.0).astype(F32)

    loads = [
        pltpu.make_async_copy(air_hbm, air.at[0, :, pl.ds(1, depth)], load_sem.at[0]),
        pltpu.make_async_copy(speed_hbm, speed, load_sem.at[1]),
        pltpu.make_async_copy(upwind_hbm, upwind, load_sem.at[2]),
    ]
    for load in loads:
        load.start()

    barrier = pltpu.get_barrier_semaphore()

    def greet(d, carry):
        pl.semaphore_signal(
            barrier, inc=1, device_id={"vert": lax.rem(me + d, groups)}, device_id_type=MESH
        )
        return carry

    lax.fori_loop(1, groups, greet, 0)
    for neighbour in (east, west):
        pl.semaphore_signal(barrier, inc=1, device_id={"horiz": neighbour}, device_id_type=MESH)

    plane0 = jnp.zeros((fields, breadth, span), F32)
    for slot in range(2):
        air[slot, :, 0] = plane0
        air[slot, :, depth + 1] = plane0
    in_z[0] = jnp.zeros((breadth, span), F32)

    material = mat_ref[...]
    hcoef = jnp.zeros(material.shape, F32)
    for k in range(table_ref.shape[0]):
        hcoef = jnp.where(material == k, table_ref[k], hcoef)
    layer = lax.broadcasted_iota(I32, (ROWS, walls), 0)
    surface = (layer == 0).astype(F32)
    cond8 = jnp.concatenate([cond_ref[...], jnp.zeros((1, walls), F32)], axis=0)
    h_top = surface * hcoef
    p = wall_ref[...]
    e = surface
    values = [face_ref[...].astype(F32), hcoef]
    for step in range(steps):
        values.append(p[0:1])
        if step < steps - 1:
            p = wall_back(p, cond8) - h_top * p
    for _ in range(steps - 2):
        e = wall_back(e, cond8) - h_top * e
        values.append(e[0:1])
    values = jnp.concatenate(values, axis=0)

    owners = owner_ref[...]
    owned = (lax.broadcasted_iota(I32, (groups, walls), 0) == owners).astype(F32)
    block = 2 * LANES
    blocks = walls // block
    stacked = jnp.concatenate(
        [owned[:, k * block : (k + 1) * block] for k in range(blocks)], axis=0
    )
    lower = (
        lax.broadcasted_iota(I32, (block, block), 0) < lax.broadcasted_iota(I32, (block, block), 1)
    ).astype(F32)
    before = dot(stacked.astype(BF16), lower.astype(BF16))
    totals = jnp.sum(stacked, axis=1, keepdims=True)
    offset = jnp.zeros((groups, 1), F32)
    ranks = []
    for k in range(blocks):
        part = slice(k * groups, (k + 1) * groups)
        ranks.append(
            jnp.sum(stacked[part] * (before[part] + offset), axis=0, keepdims=True)
        )
        offset = offset + totals[part]
    ranks = jnp.concatenate(ranks, axis=1).astype(I32)
    rank_hot[...] = (
        (lax.broadcasted_iota(I32, (cap, walls), 0) == ranks).astype(F32).astype(BF16)
    )
    for s, piece in enumerate(split(values, 3)):
        for b in range(0, groups, 2):
            pair = jnp.concatenate([piece * owned[b : b + 1], piece * owned[b + 1 : b + 2]], axis=0)
            parts_ref[pl.ds((s * groups + b) * ROWS, 2 * ROWS), :] = pair.astype(BF16)
    placed = dot_nt(parts_ref[...], rank_hot[...])
    n = groups * ROWS
    parcel[...] = placed[:n] + placed[n : 2 * n] + placed[2 * n :]
    served[pl.ds(pl.multiple_of(me * ROWS, ROWS), ROWS), :] = parcel[
        pl.ds(pl.multiple_of(me * ROWS, ROWS), ROWS), :
    ]
    result[...] = jnp.zeros_like(result)

    pl.semaphore_wait(barrier, groups + 1)

    def parcel_copy(d, src, dst, send, recv):
        to = lax.rem(me + d, groups)
        return pltpu.make_async_remote_copy(
            src_ref=src.at[pl.ds(pl.multiple_of(to * ROWS, ROWS), ROWS)],
            dst_ref=dst.at[pl.ds(pl.multiple_of(me * ROWS, ROWS), ROWS)],
            send_sem=send.at[d],
            recv_sem=recv.at[d],
            device_id={"vert": to},
            device_id_type=MESH,
        )

    def send_parcel(d, carry):
        parcel_copy(d, parcel, served, parcel_send, parcel_recv).start()
        return carry

    lax.fori_loop(1, groups, send_parcel, 0)

    def halo_copies(step, slot):
        return [
            pltpu.make_async_remote_copy(
                src_ref=src,
                dst_ref=dst,
                send_sem=halo_send.at[step, k],
                recv_sem=halo_recv.at[step, k],
                device_id=to,
                device_id_type=MESH,
            )
            for k, (src, dst, to) in enumerate(
                [
                    (air.at[slot, :, depth], halo_z.at[step, 0], {"vert": above}),
                    (air.at[slot, :, 1], halo_z.at[step, 1], {"vert": below}),
                    (edge_x.at[step, 1], halo_x.at[step, 0], {"horiz": east}),
                    (edge_x.at[step, 0], halo_x.at[step, 1], {"horiz": west}),
                ]
            )
        ]

    def split_plane(slot, z):
        plane = air[slot, 0, z + 1]
        hi = plane.astype(BF16)
        at = pl.ds(pl.multiple_of(z * breadth, breadth), breadth)
        field_hi[at, :] = hi
        field_lo[at, :] = (plane - hi.astype(F32)).astype(BF16)

    loads[0].wait()

    def pack_first(z, carry):
        for f in range(fields):
            edge_x[0, 0, f, pl.ds(z, 1), :] = air[0, f, z + 1, 0:1, :]
            edge_x[0, 1, f, pl.ds(z, 1), :] = air[0, f, z + 1, breadth - 1 : breadth, :]
        split_plane(0, z)
        return carry

    lax.fori_loop(0, depth, pack_first, 0)
    for copy in halo_copies(0, 0):
        copy.start()

    loads[1].wait()
    loads[2].wait()
    row_id = lax.broadcasted_iota(I32, (breadth, span), 0)
    lane_id = lax.broadcasted_iota(I32, (breadth, span), 1)

    def coefficients(z, carry):
        out, inn = [], []
        for d in range(3):
            s = speed[d, z]
            o = s * upwind[d, z].astype(F32)
            out.append(o)
            inn.append(s - o)
            speed[d, z] = o
        in_z[z + 1] = -inn[0]
        in_x_last[pl.ds(z, 1), :] = -inn[1][breadth - 1 : breadth]
        out_x_last[pl.ds(z, 1), :] = out[1][breadth - 1 : breadth]
        low_x = jnp.where(row_id == 0, 0.0, pltpu.roll(-inn[1], 1, 0))
        low_y = jnp.where(lane_id == 0, 0.0, pltpu.roll(-inn[2], 1, 1))
        in_x[z] = low_x
        in_y[z] = low_y
        centre_c[z] = 1.0 - (out[0] + out[1] + out[2]) - (in_z[z] + low_x + low_y)
        return carry

    lax.fori_loop(0, depth, coefficients, 0)
    in_copies = [
        pltpu.make_async_remote_copy(
            src_ref=src,
            dst_ref=dst,
            send_sem=in_send.at[k],
            recv_sem=in_recv.at[k],
            device_id=to,
            device_id_type=MESH,
        )
        for k, (src, dst, to) in enumerate(
            [
                (in_z.at[depth], in_z_halo, {"vert": above}),
                (in_x_last, in_x_halo, {"horiz": east}),
            ]
        )
    ]
    for copy in in_copies:
        copy.start()

    def wait_parcel(d, carry):
        parcel_copy(d, parcel, served, parcel_send, parcel_recv).wait()
        return carry

    lax.fori_loop(1, groups, wait_parcel, 0)

    def one_hots(s, carry):
        cell = served[pl.ds(pl.multiple_of(s * ROWS, ROWS), ROWS), :][0:1].astype(I32)
        row_hot[s] = (
            (lax.broadcasted_iota(I32, (rows, cap), 0) == cell // span).astype(F32).astype(BF16)
        )
        col_hot[s] = (
            (lax.broadcasted_iota(I32, (span, cap), 0) == cell % span).astype(F32).astype(BF16)
        )
        return carry

    lax.fori_loop(0, groups, one_hots, 0)

    sub8 = lax.broadcasted_iota(I32, (SUBS, LANES), 0)
    lane8 = lax.broadcasted_iota(I32, (SUBS, LANES), 1)

    def stencil(cur, new, z):
        zero = jnp.zeros((SUBS, LANES), F32)
        first_lane, last_lane = lane8 == 0, lane8 == LANES - 1
        first_sub, last_sub = sub8 == 0, sub8 == SUBS - 1
        for f in range(fields):
            kappa = kappa_ref[f]
            tile = {}
            for i in range(x_tiles):
                for h in range(2):
                    tile[i, h] = air[
                        cur, f, z + 1, SUBS * i : SUBS * (i + 1), LANES * h : LANES * (h + 1)
                    ]
            down = {k: pltpu.roll(t, 1, 0) for k, t in tile.items()}
            up = {k: pltpu.roll(t, SUBS - 1, 0) for k, t in tile.items()}
            for i in range(x_tiles):
                right = [pltpu.roll(tile[i, h], 1, 1) for h in range(2)]
                left = [pltpu.roll(tile[i, h], LANES - 1, 1) for h in range(2)]
                south = [jnp.where(first_lane, 0.0, right[0]), jnp.where(first_lane, *right)]
                north = [
                    jnp.where(last_lane, left[1], left[0]),
                    jnp.where(last_lane, 0.0, left[1]),
                ]
                for h in range(2):
                    at = (slice(SUBS * i, SUBS * (i + 1)), slice(LANES * h, LANES * (h + 1)))
                    m_west = jnp.where(first_sub, down[i - 1, h] if i else zero, down[i, h])
                    m_east = jnp.where(
                        last_sub, up[i + 1, h] if i + 1 < x_tiles else zero, up[i, h]
                    )
                    total = (centre_c[(z,) + at] - 6.0 * kappa) * tile[i, h]
                    total += (speed[(0, z) + at] + kappa) * air[(cur, f, z + 2) + at]
                    total += (in_z[(z,) + at] + kappa) * air[(cur, f, z) + at]
                    total += (speed[(1, z) + at] + kappa) * m_east
                    total += (in_x[(z,) + at] + kappa) * m_west
                    total += (speed[(2, z) + at] + kappa) * north[h]
                    total += (in_y[(z,) + at] + kappa) * south[h]
                    air[(new, f, z + 1) + at] = total

    def gather(s):
        cell = served[pl.ds(pl.multiple_of(s * ROWS, ROWS), ROWS), :][0:1].astype(I32)
        hot = col_hot[s]
        picked = dot(field_hi[...], hot) + dot(field_lo[...], hot)
        mask = lax.broadcasted_iota(I32, (rows, cap), 0) == cell // span
        return jnp.sum(jnp.where(mask, picked, 0.0), axis=0, keepdims=True)

    def scatter(step, s, fetched):
        at = pl.ds(pl.multiple_of(s * ROWS, ROWS), ROWS)
        wall = served[at, :]
        h = wall[1:2]
        half = RATIO * fetched * h
        flow = h * wall[2 + step : 3 + step] - half
        result[pl.ds(s * ROWS + step, 1), :] = flow
        if step + 1 < steps:
            later = [wall[k : k + 1] for k in range(3 + step)]
            for k in range(step + 1, steps):
                g = steps + k - step
                seen = half if k == step + 1 else half * wall[g : g + 1]
                later.append(wall[2 + k : 3 + k] + seen)
            later += [wall[k : k + 1] for k in range(2 + steps, ROWS)]
            served[at, :] = jnp.concatenate(later, axis=0)
        hi = flow.astype(BF16)
        lo = (flow - hi.astype(F32)).astype(BF16)
        hot = col_hot[s]
        where = row_hot[s]
        added[...] += dot_nt(where, hot * hi) + dot_nt(where, hot * lo)

    def return_copy(d):
        return parcel_copy(d, result, returned, return_send, return_recv)

    for step in range(steps):
        cur, new = step % 2, (step + 1) % 2
        last = step == steps - 1
        added[...] = jnp.zeros_like(added)

        def body(s, fetched, step=step, cur=cur, new=new):
            following = gather(lax.rem(s + 1, groups))
            scatter(step, s, fetched)
            return following

        lax.fori_loop(0, groups, body, gather(0))

        def body_z(z, carry, cur=cur, new=new):
            stencil(cur, new, z)
            return carry

        lax.fori_loop(0, depth, body_z, 0)

        if last:
            def send_back(d, carry):
                return_copy(d).start()
                return carry

            lax.fori_loop(1, groups, send_back, 0)
            own = pl.ds(pl.multiple_of(me * ROWS, ROWS), ROWS)
            returned[own, :] = result[own, :]

        for copy in halo_copies(step, cur):
            copy.wait()
        if step == 0:
            for copy in in_copies:
                copy.wait()
            in_z_halo[...] = in_z_halo[...] * has_below
            in_x_halo[...] = in_x_halo[...] * has_west
        for f in range(fields):
            kappa = kappa_ref[f]
            beyond = halo_z[step, 0, f] * has_below
            air[new, f, 1] += kappa * beyond + in_z_halo[...] * (beyond - air[cur, f, 1])
            beyond = halo_z[step, 1, f] * has_above
            air[new, f, depth] += (speed[0, depth - 1] + kappa) * beyond
            beyond = halo_x[step, 0, f] * has_west
            fix_x[0, f] = kappa * beyond + in_x_halo[...] * (beyond - edge_x[step, 0, f])
            beyond = halo_x[step, 1, f] * has_east
            fix_x[1, f] = (out_x_last[...] + kappa) * beyond

        def finish(z, carry, step=step, new=new, last=last):
            at = pl.ds(pl.multiple_of(z * breadth, breadth), breadth)
            air[new, 0, z + 1] += added[at, :]
            for f in range(fields):
                low = air[new, f, z + 1, 0:1, :] + fix_x[0, f, pl.ds(z, 1), :]
                high = (
                    air[new, f, z + 1, breadth - 1 : breadth, :] + fix_x[1, f, pl.ds(z, 1), :]
                )
                air[new, f, z + 1, 0:1, :] = low
                air[new, f, z + 1, breadth - 1 : breadth, :] = high
                if not last:
                    edge_x[step + 1, 0, f, pl.ds(z, 1), :] = low
                    edge_x[step + 1, 1, f, pl.ds(z, 1), :] = high
            if not last:
                split_plane(new, z)
            return carry

        lax.fori_loop(0, depth, finish, 0)
        if not last:
            for copy in halo_copies(step + 1, new):
                copy.start()

    store = pltpu.make_async_copy(
        air.at[steps % 2, :, pl.ds(1, depth)], air_out, store_sem
    )
    store.start()

    def wait_back(d, carry):
        return_copy(d).wait()
        return carry

    lax.fori_loop(1, groups, wait_back, 0)
    back = returned[...]
    placed = dot(jnp.concatenate(split(back, 3), axis=0).astype(BF16), rank_hot[...])
    placed = placed[:n] + placed[n : 2 * n] + placed[2 * n :]
    flows = jnp.zeros((ROWS, walls), F32)
    for b in range(groups):
        flows = flows + owned[b : b + 1] * placed[b * ROWS : (b + 1) * ROWS]
    p = wall_ref[...]
    grad = jnp.zeros((ROWS, walls), F32)
    for step in range(steps):
        saved = saved_ref[steps - 1 - step]
        grad = grad - (pltpu.roll(saved, ROWS - 1, 0) - saved) * (pltpu.roll(p, ROWS - 1, 0) - p)
        p = wall_back(p, cond8) - surface * flows[step : step + 1]
    wall_out[...] = p
    grad_out[...] = grad[: ROWS - 1]
    store.wait()


def per_device(
    air_seed,
    wall_seed,
    speed,
    upwind,
    diffusivity,
    conductivity,
    wall_saved,
    heat_table,
    interface,
    owner,
    material,
):
    groups, columns = lax.axis_size("vert"), lax.axis_size("horiz")
    steps = wall_saved.shape[0]
    walls = interface.shape[0]
    cap = walls // 4
    fields, depth, breadth, span = air_seed.shape
    rows = depth * breadth
    vmem = pl.BlockSpec(memory_space=pltpu.VMEM)
    smem = pl.BlockSpec(memory_space=pltpu.SMEM)
    hbm = pl.BlockSpec(memory_space=pl.ANY)
    dma = pltpu.SemaphoreType.DMA
    plane = (breadth, span)
    brick = (depth, breadth, span)
    side = (depth, span)
    scratch = [
        pltpu.VMEM((2, fields, depth + 2) + plane, F32),
        pltpu.VMEM((3,) + brick, F32),
        pltpu.VMEM((3,) + brick, I32),
        pltpu.VMEM((depth + 1,) + plane, F32),
        pltpu.VMEM(brick, F32),
        pltpu.VMEM(brick, F32),
        pltpu.VMEM(brick, F32),
        pltpu.VMEM(side, F32),
        pltpu.VMEM(side, F32),
        pltpu.VMEM(plane, F32),
        pltpu.VMEM(side, F32),
        pltpu.VMEM((steps, 2, fields) + plane, F32),
        pltpu.VMEM((steps, 2, fields) + side, F32),
        pltpu.VMEM((steps, 2, fields) + side, F32),
        pltpu.VMEM((2, fields) + side, F32),
        pltpu.VMEM((rows, span), BF16),
        pltpu.VMEM((rows, span), BF16),
        pltpu.VMEM((groups, rows, cap), BF16),
        pltpu.VMEM((groups, span, cap), BF16),
        pltpu.VMEM((rows, span), F32),
        pltpu.VMEM((3 * groups * ROWS, walls), BF16),
        pltpu.VMEM((cap, walls), BF16),
        pltpu.VMEM((groups * ROWS, cap), F32),
        pltpu.VMEM((groups * ROWS, cap), F32),
        pltpu.VMEM((groups * ROWS, cap), F32),
        pltpu.VMEM((groups * ROWS, cap), F32),
        dma((3,)),
        dma(()),
        dma((2,)),
        dma((2,)),
        dma((steps, 4)),
        dma((steps, 4)),
        dma((groups,)),
        dma((groups,)),
        dma((groups,)),
        dma((groups,)),
    ]
    return pl.pallas_call(
        functools.partial(kernel, (steps, groups, columns)),
        out_shape=(
            jax.ShapeDtypeStruct(air_seed.shape, F32),
            jax.ShapeDtypeStruct(wall_seed.shape, F32),
            jax.ShapeDtypeStruct(conductivity.shape, F32),
        ),
        in_specs=[smem, smem] + [vmem] * 6 + [hbm] * 3,
        out_specs=(hbm, vmem, vmem),
        scratch_shapes=scratch,
        compiler_params=pltpu.CompilerParams(
            collective_id=0, has_side_effects=True, vmem_limit_bytes=48 * 1024 * 1024
        ),
        cost_estimate=pl.CostEstimate(
            flops=2 * steps * 4 * groups * cap * rows * span,
            bytes_accessed=40 * rows * span,
            transcendentals=0,
        ),
    )(
        diffusivity,
        heat_table,
        wall_seed,
        conductivity,
        wall_saved,
        interface.reshape(1, walls),
        owner.reshape(1, walls),
        material.reshape(1, walls),
        air_seed,
        speed,
        upwind,
    )


def solution(mesh):
    air = P(None, "vert", "horiz", None)
    wall = P(None, ("horiz", "vert"))
    column = P(("horiz", "vert"))
    return jax.shard_map(
        per_device,
        mesh=mesh,
        in_specs=(
            air,
            wall,
            air,
            air,
            P(),
            wall,
            P(None, None, ("horiz", "vert")),
            P(),
            column,
            P(("horiz", "vert"), None),
            column,
        ),
        out_specs=(air, wall, wall),
        check_vma=False,
    )
```

```python
import functools

import jax
import jax.numpy as jnp
from jax import lax
from jax.experimental import pallas as pl
from jax.experimental.pallas import tpu as pltpu
from jax.sharding import PartitionSpec as P

F32, BF16, I32 = jnp.float32, jnp.bfloat16, jnp.int32
MESH = pl.DeviceIdType.MESH
LANES, SUBS = 128, 8
RATIO = 0.5
VMEM_BYTES = 64 * 1024 * 1024 - 64 * 1024
ROWS = 8
NT = (((1,), (1,)), ((), ()))


def dot(a, b):
    return jnp.dot(a, b, preferred_element_type=F32)


def dot_nt(a, b):
    return lax.dot_general(a, b, NT, preferred_element_type=F32)


def split(value, parts):
    pieces = []
    for _ in range(parts):
        piece = value.astype(BF16).astype(F32)
        pieces.append(piece)
        value = value - piece
    return pieces


def wall_back(p, cond8):
    flux = cond8 * (pltpu.roll(p, ROWS - 1, 0) - p)
    return p + flux - pltpu.roll(flux, 1, 0)


def kernel(
    dims,
    kappa_ref,
    table_ref,
    wall_hbm,
    cond_hbm,
    saved_hbm,
    face_hbm,
    owner_hbm,
    mat_hbm,
    air_hbm,
    speed_hbm,
    upwind_hbm,
    air_out,
    wall_out,
    grad_out,
    wall_ref,
    cond_ref,
    saved_ref,
    face_ref,
    owner_ref,
    mat_ref,
    air,
    speed,
    upwind,
    in_z,
    in_x,
    in_y,
    centre_c,
    out_x_last,
    in_x_last,
    in_z_halo,
    in_x_halo,
    halo_z,
    halo_x,
    edge_x,
    fix_x,
    field_t,
    row_hot,
    col_hot,
    flows_ref,
    added,
    parts_ref,
    rank_hot,
    owned_ref,
    parcel,
    served,
    result,
    returned,
    wall_res,
    grad_res,
    load_sem,
    store_sem,
    in_send,
    in_recv,
    halo_send,
    halo_recv,
    parcel_send,
    parcel_recv,
    return_send,
    return_recv,
):
    steps, groups, columns = dims
    fields, depth, breadth, span = air_out.shape
    walls = face_ref.shape[1]
    cap = rank_hot.shape[0]
    rows = depth * breadth
    x_tiles = breadth // SUBS
    chunks, _, chunk = served.shape
    per_chunk = chunk // cap
    me = lax.axis_index("vert")
    col = lax.axis_index("horiz")
    above, below = lax.rem(me + 1, groups), lax.rem(me + groups - 1, groups)
    east, west = lax.rem(col + 1, columns), lax.rem(col + columns - 1, columns)
    has_below = jnp.where(me > 0, 1.0, 0.0).astype(F32)
    has_above = jnp.where(me < groups - 1, 1.0, 0.0).astype(F32)
    has_west = jnp.where(col > 0, 1.0, 0.0).astype(F32)
    has_east = jnp.where(col < columns - 1, 1.0, 0.0).astype(F32)

    barrier = pltpu.get_barrier_semaphore()

    def greet(d, carry):
        pl.semaphore_signal(
            barrier, inc=1, device_id={"vert": lax.rem(me + d, groups)}, device_id_type=MESH
        )
        return carry

    loads = [
        pltpu.make_async_copy(src, dst, load_sem.at[k])
        for k, (src, dst) in enumerate(
            [
                (owner_hbm, owner_ref),
                (face_hbm, face_ref),
                (mat_hbm, mat_ref),
                (wall_hbm, wall_ref),
                (cond_hbm, cond_ref),
                (air_hbm, air.at[0, :, pl.ds(1, depth)]),
                (speed_hbm, speed),
                (upwind_hbm, upwind),
                (saved_hbm, saved_ref),
            ]
        )
    ]
    for load in loads:
        load.start()
    lax.fori_loop(1, groups, greet, 0)
    for neighbour in (east, west):
        pl.semaphore_signal(barrier, inc=1, device_id={"horiz": neighbour}, device_id_type=MESH)

    plane0 = jnp.zeros((fields, breadth, span), F32)
    for slot in range(2):
        air[slot, :, 0] = plane0
        air[slot, :, depth + 1] = plane0
    in_z[0] = jnp.zeros((breadth, span), F32)
    result[...] = jnp.zeros_like(result)

    loads[0].wait()
    owned = (lax.broadcasted_iota(I32, (groups, walls), 0) == owner_ref[...]).astype(F32)
    owned_ref[...] = owned
    block = 2 * LANES
    blocks = walls // block
    stacked = jnp.concatenate(
        [owned[:, k * block : (k + 1) * block] for k in range(blocks)], axis=0
    )
    lower = (
        lax.broadcasted_iota(I32, (block, block), 0) < lax.broadcasted_iota(I32, (block, block), 1)
    ).astype(F32)
    before = dot(stacked.astype(BF16), lower.astype(BF16))
    totals = jnp.sum(stacked, axis=1, keepdims=True)
    offset = jnp.zeros((groups, 1), F32)
    ranks = []
    for k in range(blocks):
        part = slice(k * groups, (k + 1) * groups)
        ranks.append(
            jnp.sum(stacked[part] * (before[part] + offset), axis=0, keepdims=True)
        )
        offset = offset + totals[part]
    ranks = jnp.concatenate(ranks, axis=1).astype(I32)
    rank_hot[...] = (
        (lax.broadcasted_iota(I32, (cap, walls), 0) == ranks).astype(F32).astype(BF16)
    )

    for load in loads[1:5]:
        load.wait()
    material = mat_ref[...]
    hcoef = jnp.zeros(material.shape, F32)
    for k in range(table_ref.shape[0]):
        hcoef = jnp.where(material == k, table_ref[k], hcoef)
    layer = lax.broadcasted_iota(I32, (ROWS, walls), 0)
    surface = (layer == 0).astype(F32)
    cond8 = jnp.concatenate([cond_ref[...], jnp.zeros((1, walls), F32)], axis=0)
    h_top = surface * hcoef
    p = wall_ref[...]
    e = surface
    values = [face_ref[...].astype(F32), hcoef]
    for step in range(steps):
        values.append(p[0:1])
        if step < steps - 1:
            p = wall_back(p, cond8) - h_top * p
    for _ in range(steps - 2):
        e = wall_back(e, cond8) - h_top * e
        values.append(e[0:1])
    values = jnp.concatenate(values, axis=0)
    for s, piece in enumerate(split(values, 3)):
        for b in range(0, groups, 2):
            pair = jnp.concatenate([piece * owned[b : b + 1], piece * owned[b + 1 : b + 2]], axis=0)
            parts_ref[pl.ds((s * groups + b) * ROWS, 2 * ROWS), :] = pair.astype(BF16)
    placed = dot_nt(parts_ref[...], rank_hot[...])
    n = groups * ROWS
    parcel[...] = placed[:n] + placed[n : 2 * n] + placed[2 * n :]

    def at_rows(k):
        return pl.ds(pl.multiple_of(k * ROWS, ROWS), ROWS)

    def at_lanes(k):
        return pl.ds(pl.multiple_of(lax.rem(k, per_chunk) * cap, cap), cap)

    served[lax.div(me, per_chunk), :, at_lanes(me)] = parcel[at_rows(me), :]

    pl.semaphore_wait(barrier, groups + 1)

    def parcel_copy(d):
        to = lax.rem(me + d, groups)
        return pltpu.make_async_remote_copy(
            src_ref=parcel.at[at_rows(to)],
            dst_ref=served.at[lax.div(me, per_chunk), :, at_lanes(me)],
            send_sem=parcel_send.at[d],
            recv_sem=parcel_recv.at[d],
            device_id={"vert": to},
            device_id_type=MESH,
        )

    def return_copy(d):
        to = lax.rem(me + d, groups)
        return pltpu.make_async_remote_copy(
            src_ref=result.at[lax.div(to, per_chunk), :, at_lanes(to)],
            dst_ref=returned.at[at_rows(me)],
            send_sem=return_send.at[d],
            recv_sem=return_recv.at[d],
            device_id={"vert": to},
            device_id_type=MESH,
        )

    def each(copy, act):
        def body(d, carry):
            act(copy(d))
            return carry

        lax.fori_loop(1, groups, body, 0)

    each(parcel_copy, lambda copy: copy.start())

    def halo_copies(step, slot):
        return [
            pltpu.make_async_remote_copy(
                src_ref=src,
                dst_ref=dst,
                send_sem=halo_send.at[step, k],
                recv_sem=halo_recv.at[step, k],
                device_id=to,
                device_id_type=MESH,
            )
            for k, (src, dst, to) in enumerate(
                [
                    (air.at[slot, :, depth], halo_z.at[step, 0], {"vert": above}),
                    (air.at[slot, :, 1], halo_z.at[step, 1], {"vert": below}),
                    (edge_x.at[step, 1], halo_x.at[step, 0], {"horiz": east}),
                    (edge_x.at[step, 0], halo_x.at[step, 1], {"horiz": west}),
                ]
            )
        ]

    planes = LANES // breadth

    def split_field(slot):
        def body(k, carry):
            block = air[slot, 0, pl.ds(1 + k * planes, planes)].reshape(LANES, span).T
            hi = block.astype(BF16)
            field_t[:, pl.ds(pl.multiple_of(k * LANES, LANES), LANES)] = hi
            field_t[:, pl.ds(pl.multiple_of(rows + k * LANES, LANES), LANES)] = (
                block - hi.astype(F32)
            ).astype(BF16)
            return carry

        lax.fori_loop(0, depth // planes, body, 0)

    loads[5].wait()

    def pack_first(z, carry):
        for f in range(fields):
            edge_x[0, 0, f, pl.ds(z, 1), :] = air[0, f, z + 1, 0:1, :]
            edge_x[0, 1, f, pl.ds(z, 1), :] = air[0, f, z + 1, breadth - 1 : breadth, :]
        return carry

    lax.fori_loop(0, depth, pack_first, 0)
    for copy in halo_copies(0, 0):
        copy.start()
    split_field(0)

    loads[6].wait()
    loads[7].wait()
    row_id = lax.broadcasted_iota(I32, (breadth, span), 0)
    lane_id = lax.broadcasted_iota(I32, (breadth, span), 1)

    def coefficients(z, carry):
        out, inn = [], []
        for d in range(3):
            s = speed[d, z]
            o = s * upwind[d, z].astype(F32)
            out.append(o)
            inn.append(s - o)
            speed[d, z] = o
        in_z[z + 1] = -inn[0]
        in_x_last[pl.ds(z, 1), :] = -inn[1][breadth - 1 : breadth]
        out_x_last[pl.ds(z, 1), :] = out[1][breadth - 1 : breadth]
        low_x = jnp.where(row_id == 0, 0.0, pltpu.roll(-inn[1], 1, 0))
        low_y = jnp.where(lane_id == 0, 0.0, pltpu.roll(-inn[2], 1, 1))
        in_x[z] = low_x
        in_y[z] = low_y
        centre_c[z] = 1.0 - (out[0] + out[1] + out[2]) - (in_z[z] + low_x + low_y)
        return carry

    lax.fori_loop(0, depth, coefficients, 0)
    in_copies = [
        pltpu.make_async_remote_copy(
            src_ref=src,
            dst_ref=dst,
            send_sem=in_send.at[k],
            recv_sem=in_recv.at[k],
            device_id=to,
            device_id_type=MESH,
        )
        for k, (src, dst, to) in enumerate(
            [
                (in_z.at[depth], in_z_halo, {"vert": above}),
                (in_x_last, in_x_halo, {"horiz": east}),
            ]
        )
    ]
    for copy in in_copies:
        copy.start()

    sub8 = lax.broadcasted_iota(I32, (SUBS, LANES), 0)
    lane8 = lax.broadcasted_iota(I32, (SUBS, LANES), 1)

    def stencil(cur, new, z):
        zero = jnp.zeros((SUBS, LANES), F32)
        first_lane, last_lane = lane8 == 0, lane8 == LANES - 1
        first_sub, last_sub = sub8 == 0, sub8 == SUBS - 1
        for f in range(fields):
            kappa = kappa_ref[f]
            tile = {}
            for i in range(x_tiles):
                for h in range(2):
                    tile[i, h] = air[
                        cur, f, z + 1, SUBS * i : SUBS * (i + 1), LANES * h : LANES * (h + 1)
                    ]
            down = {k: pltpu.roll(t, 1, 0) for k, t in tile.items()}
            up = {k: pltpu.roll(t, SUBS - 1, 0) for k, t in tile.items()}
            for i in range(x_tiles):
                right = [pltpu.roll(tile[i, h], 1, 1) for h in range(2)]
                left = [pltpu.roll(tile[i, h], LANES - 1, 1) for h in range(2)]
                south = [jnp.where(first_lane, 0.0, right[0]), jnp.where(first_lane, *right)]
                north = [
                    jnp.where(last_lane, left[1], left[0]),
                    jnp.where(last_lane, 0.0, left[1]),
                ]
                for h in range(2):
                    at = (slice(SUBS * i, SUBS * (i + 1)), slice(LANES * h, LANES * (h + 1)))
                    m_west = jnp.where(first_sub, down[i - 1, h] if i else zero, down[i, h])
                    m_east = jnp.where(
                        last_sub, up[i + 1, h] if i + 1 < x_tiles else zero, up[i, h]
                    )
                    total = (centre_c[(z,) + at] - 6.0 * kappa) * tile[i, h]
                    total += (speed[(0, z) + at] + kappa) * air[(cur, f, z + 2) + at]
                    total += (in_z[(z,) + at] + kappa) * air[(cur, f, z) + at]
                    total += (speed[(1, z) + at] + kappa) * m_east
                    total += (in_x[(z,) + at] + kappa) * m_west
                    total += (speed[(2, z) + at] + kappa) * north[h]
                    total += (in_y[(z,) + at] + kappa) * south[h]
                    air[(new, f, z + 1) + at] = total

    def stencil_first(z, carry):
        stencil(0, 1, z)
        return carry

    lax.fori_loop(0, depth, stencil_first, 0)
    each(parcel_copy, lambda copy: copy.wait())

    def one_hots(c, carry):
        cell = served[c, 0:1, :].astype(I32)
        hot = (lax.broadcasted_iota(I32, (rows, chunk), 0) == cell // span).astype(F32).astype(BF16)
        row_hot[c, :rows] = hot
        row_hot[c, rows:] = hot
        col_hot[c] = (
            (lax.broadcasted_iota(I32, (span, chunk), 0) == cell % span).astype(F32).astype(BF16)
        )
        return carry

    lax.fori_loop(0, chunks, one_hots, 0)

    def gather(step, c):
        picked = dot(field_t[...], row_hot[c])
        wall = served[c]
        y = wall[0:1].astype(I32) % span
        mask = lax.broadcasted_iota(I32, (span, chunk), 0) == y
        fetched = jnp.sum(jnp.where(mask, picked, 0.0), axis=0, keepdims=True)
        h = wall[1:2]
        half = RATIO * fetched * h
        flow = h * wall[2 + step : 3 + step] - half
        flows_ref[pl.ds(c, 1), :] = flow
        result[c, step : step + 1, :] = flow
        if step + 1 < steps:
            later = [wall[k : k + 1] for k in range(3 + step)]
            for k in range(step + 1, steps):
                g = steps + k - step
                seen = half if k == step + 1 else half * wall[g : g + 1]
                later.append(wall[2 + k : 3 + k] + seen)
            later += [wall[k : k + 1] for k in range(2 + steps, ROWS)]
            served[c] = jnp.concatenate(later, axis=0)

    def scatter(c):
        flow = flows_ref[pl.ds(c, 1), :]
        hi = flow.astype(BF16)
        lo = (flow - hi.astype(F32)).astype(BF16)
        hot = col_hot[c]
        where = row_hot[c, :rows]
        added[...] += dot_nt(where, hot * hi) + dot_nt(where, hot * lo)

    def beyond_z(step, f):
        cur, new = step % 2, (step + 1) % 2
        kappa = kappa_ref[f]
        beyond = halo_z[step, 0, f] * has_below
        air[new, f, 1] += kappa * beyond + in_z_halo[...] * (beyond - air[cur, f, 1])
        beyond = halo_z[step, 1, f] * has_above
        air[new, f, depth] += (speed[0, depth - 1] + kappa) * beyond
        beyond = halo_x[step, 0, f] * has_west
        fix_x[0, f] = kappa * beyond + in_x_halo[...] * (beyond - edge_x[step, 0, f])
        beyond = halo_x[step, 1, f] * has_east
        fix_x[1, f] = (out_x_last[...] + kappa) * beyond

    def finish(step, chosen):
        new = (step + 1) % 2
        for f in chosen:
            beyond_z(step, f)

        def body(z, carry):
            at = pl.ds(pl.multiple_of(z * breadth, breadth), breadth)
            if 0 in chosen:
                air[new, 0, z + 1] += added[at, :]
            for f in chosen:
                low = air[new, f, z + 1, 0:1, :] + fix_x[0, f, pl.ds(z, 1), :]
                high = (
                    air[new, f, z + 1, breadth - 1 : breadth, :] + fix_x[1, f, pl.ds(z, 1), :]
                )
                air[new, f, z + 1, 0:1, :] = low
                air[new, f, z + 1, breadth - 1 : breadth, :] = high
                if step + 1 < steps:
                    edge_x[step + 1, 0, f, pl.ds(z, 1), :] = low
                    edge_x[step + 1, 1, f, pl.ds(z, 1), :] = high
            return carry

        lax.fori_loop(0, depth, body, 0)

    def wait_halos(step):
        for copy in halo_copies(step, step % 2):
            copy.wait()
        if step == 0:
            for copy in in_copies:
                copy.wait()
            in_z_halo[...] = in_z_halo[...] * has_below
            in_x_halo[...] = in_x_halo[...] * has_west

    def store(f):
        return pltpu.make_async_copy(
            air.at[steps % 2, f, pl.ds(1, depth)], air_out.at[f], store_sem.at[f]
        )

    for step in range(steps):
        cur, new = step % 2, (step + 1) % 2
        last = step == steps - 1
        in_gather = 0 if step == 0 else depth // chunks if last else depth // chunks // 2
        in_scatter = 0 if step == 0 else depth // chunks - in_gather

        def body_gather(c, carry, step=step, cur=cur, new=new, count=in_gather):
            gather(step, c)
            for k in range(count):
                stencil(cur, new, c * count + k)
            return carry

        lax.fori_loop(0, chunks, body_gather, 0)
        if last:
            each(return_copy, lambda copy: copy.start())
            returned[at_rows(me), :] = result[lax.div(me, per_chunk), :, at_lanes(me)]
            wait_halos(step)
            finish(step, range(1, fields))
            for f in range(1, fields):
                store(f).start()
        added[...] = jnp.zeros_like(added)

        def body_scatter(c, carry, cur=cur, new=new, count=in_scatter, first=in_gather * chunks):
            scatter(c)
            for k in range(count):
                stencil(cur, new, first + c * count + k)
            return carry

        lax.fori_loop(0, chunks, body_scatter, 0)
        if last:
            finish(step, range(1))
            store(0).start()
        else:
            wait_halos(step)
            finish(step, range(fields))
            for copy in halo_copies(step + 1, new):
                copy.start()
            split_field(new)

    each(return_copy, lambda copy: copy.wait())
    loads[8].wait()
    placed = dot(jnp.concatenate(split(returned[...], 3), axis=0).astype(BF16), rank_hot[...])
    placed = placed[:n] + placed[n : 2 * n] + placed[2 * n :]
    flows = jnp.zeros((ROWS, walls), F32)
    for b in range(groups):
        flows = flows + owned_ref[b : b + 1] * placed[b * ROWS : (b + 1) * ROWS]
    p = wall_ref[...]
    cond8 = jnp.concatenate([cond_ref[...], jnp.zeros((1, walls), F32)], axis=0)
    grad = jnp.zeros((ROWS, walls), F32)
    for step in range(steps):
        saved = saved_ref[steps - 1 - step]
        grad = grad - (pltpu.roll(saved, ROWS - 1, 0) - saved) * (pltpu.roll(p, ROWS - 1, 0) - p)
        p = wall_back(p, cond8) - surface * flows[step : step + 1]
    wall_res[...] = p
    grad_res[...] = grad[: ROWS - 1]
    stores = [
        pltpu.make_async_copy(wall_res, wall_out, store_sem.at[fields]),
        pltpu.make_async_copy(grad_res, grad_out, store_sem.at[fields + 1]),
    ]
    for copy in stores:
        copy.start()
    for copy in stores + [store(f) for f in range(fields)]:
        copy.wait()


def per_device(
    air_seed,
    wall_seed,
    speed,
    upwind,
    diffusivity,
    conductivity,
    wall_saved,
    heat_table,
    interface,
    owner,
    material,
):
    groups, columns = lax.axis_size("vert"), lax.axis_size("horiz")
    steps = wall_saved.shape[0]
    walls = interface.shape[0]
    cap = walls // 4
    fields, depth, breadth, span = air_seed.shape
    rows = depth * breadth
    chunks = 2
    chunk = groups * cap // chunks
    smem = pl.BlockSpec(memory_space=pltpu.SMEM)
    hbm = pl.BlockSpec(memory_space=pl.ANY)
    dma = pltpu.SemaphoreType.DMA
    plane = (breadth, span)
    brick = (depth, breadth, span)
    side = (depth, span)
    scratch = [
        pltpu.VMEM(wall_seed.shape, F32),
        pltpu.VMEM(conductivity.shape, F32),
        pltpu.VMEM(wall_saved.shape, F32),
        pltpu.VMEM((1, walls), I32),
        pltpu.VMEM((1, walls), I32),
        pltpu.VMEM((1, walls), I32),
        pltpu.VMEM((2, fields, depth + 2) + plane, F32),
        pltpu.VMEM((3,) + brick, F32),
        pltpu.VMEM((3,) + brick, I32),
        pltpu.VMEM((depth + 1,) + plane, F32),
        pltpu.VMEM(brick, F32),
        pltpu.VMEM(brick, F32),
        pltpu.VMEM(brick, F32),
        pltpu.VMEM(side, F32),
        pltpu.VMEM(side, F32),
        pltpu.VMEM(plane, F32),
        pltpu.VMEM(side, F32),
        pltpu.VMEM((steps, 2, fields) + plane, F32),
        pltpu.VMEM((steps, 2, fields) + side, F32),
        pltpu.VMEM((steps, 2, fields) + side, F32),
        pltpu.VMEM((2, fields) + side, F32),
        pltpu.VMEM((span, 2 * rows), BF16),
        pltpu.VMEM((chunks, 2 * rows, chunk), BF16),
        pltpu.VMEM((chunks, span, chunk), BF16),
        pltpu.VMEM((chunks, chunk), F32),
        pltpu.VMEM((rows, span), F32),
        pltpu.VMEM((3 * groups * ROWS, walls), BF16),
        pltpu.VMEM((cap, walls), BF16),
        pltpu.VMEM((groups, walls), F32),
        pltpu.VMEM((groups * ROWS, cap), F32),
        pltpu.VMEM((chunks, ROWS, chunk), F32),
        pltpu.VMEM((chunks, ROWS, chunk), F32),
        pltpu.VMEM((groups * ROWS, cap), F32),
        pltpu.VMEM(wall_seed.shape, F32),
        pltpu.VMEM(conductivity.shape, F32),
        dma((9,)),
        dma((fields + 2,)),
        dma((2,)),
        dma((2,)),
        dma((steps, 4)),
        dma((steps, 4)),
        dma((groups,)),
        dma((groups,)),
        dma((groups,)),
        dma((groups,)),
    ]
    return pl.pallas_call(
        functools.partial(kernel, (steps, groups, columns)),
        out_shape=(
            jax.ShapeDtypeStruct(air_seed.shape, F32),
            jax.ShapeDtypeStruct(wall_seed.shape, F32),
            jax.ShapeDtypeStruct(conductivity.shape, F32),
        ),
        in_specs=[smem, smem] + [hbm] * 9,
        out_specs=(hbm, hbm, hbm),
        scratch_shapes=scratch,
        compiler_params=pltpu.CompilerParams(
            collective_id=0, has_side_effects=True, vmem_limit_bytes=VMEM_BYTES
        ),
        cost_estimate=pl.CostEstimate(
            flops=2 * steps * 4 * groups * cap * rows * span,
            bytes_accessed=40 * rows * span,
            transcendentals=0,
        ),
    )(
        diffusivity,
        heat_table,
        wall_seed,
        conductivity,
        wall_saved,
        interface.reshape(1, walls),
        owner.reshape(1, walls),
        material.reshape(1, walls),
        air_seed,
        speed,
        upwind,
    )


def solution(mesh):
    air = P(None, "vert", "horiz", None)
    wall = P(None, ("horiz", "vert"))
    column = P(("horiz", "vert"))
    return jax.shard_map(
        per_device,
        mesh=mesh,
        in_specs=(
            air,
            wall,
            air,
            air,
            P(),
            wall,
            P(None, None, ("horiz", "vert")),
            P(),
            column,
            P(("horiz", "vert"), None),
            column,
        ),
        out_specs=(air, wall, wall),
        check_vma=False,
    )
```

```python
import functools

import jax
import jax.numpy as jnp
from jax import lax
from jax.experimental import pallas as pl
from jax.experimental.pallas import tpu as pltpu
from jax.sharding import PartitionSpec as P

F32, BF16, I32 = jnp.float32, jnp.bfloat16, jnp.int32
MESH = pl.DeviceIdType.MESH
LANES, SUBS = 128, 8
RATIO = 0.5
UNROLL = 2
VMEM_BYTES = 64 * 1024 * 1024 - 64 * 1024
ROWS = 8
NT = (((1,), (1,)), ((), ()))


def dot(a, b):
    return jnp.dot(a, b, preferred_element_type=F32)


def dot_nt(a, b):
    return lax.dot_general(a, b, NT, preferred_element_type=F32)


def split(value, parts):
    pieces = []
    for _ in range(parts):
        piece = value.astype(BF16).astype(F32)
        pieces.append(piece)
        value = value - piece
    return pieces


def wall_back(p, cond8):
    flux = cond8 * (pltpu.roll(p, ROWS - 1, 0) - p)
    return p + flux - pltpu.roll(flux, 1, 0)


def kernel(
    dims,
    kappa_ref,
    table_ref,
    wall_hbm,
    cond_hbm,
    face_hbm,
    owner_hbm,
    mat_hbm,
    air_hbm,
    speed_hbm,
    upwind_hbm,
    air_out,
    returned_out,
    ranks_out,
    wall_ref,
    cond_ref,
    face_ref,
    owner_ref,
    mat_ref,
    air_even,
    air_odd,
    speed,
    upwind,
    in_z,
    in_x,
    in_y,
    centre_c,
    out_x_last,
    in_x_last,
    in_z_halo,
    in_x_halo,
    halo_z,
    halo_x,
    edge_x,
    fix_x,
    field_t,
    row_hot,
    col_hot,
    flows_ref,
    added,
    parts_ref,
    rank_hot,
    ranks_ref,
    parcel,
    served,
    result,
    returned,
    load_sem,
    store_sem,
    in_send,
    in_recv,
    halo_send,
    halo_recv,
    parcel_send,
    parcel_recv,
    return_send,
    return_recv,
):
    steps, groups, columns = dims
    airs = (air_even, air_odd)
    fields, depth, breadth, span = air_out.shape
    walls = face_ref.shape[1]
    cap = rank_hot.shape[0]
    rows = depth * breadth
    x_tiles = breadth // SUBS
    chunks, _, chunk = served.shape
    per_chunk = chunk // cap
    me = lax.axis_index("vert")
    col = lax.axis_index("horiz")
    above, below = lax.rem(me + 1, groups), lax.rem(me + groups - 1, groups)
    east, west = lax.rem(col + 1, columns), lax.rem(col + columns - 1, columns)
    has_below = jnp.where(me > 0, 1.0, 0.0).astype(F32)
    has_above = jnp.where(me < groups - 1, 1.0, 0.0).astype(F32)
    has_west = jnp.where(col > 0, 1.0, 0.0).astype(F32)
    has_east = jnp.where(col < columns - 1, 1.0, 0.0).astype(F32)

    barrier = pltpu.get_barrier_semaphore()

    def greet(d, carry):
        pl.semaphore_signal(
            barrier, inc=1, device_id={"vert": lax.rem(me + d, groups)}, device_id_type=MESH
        )
        return carry

    loads = [
        pltpu.make_async_copy(src, dst, load_sem.at[k])
        for k, (src, dst) in enumerate(
            [
                (owner_hbm, owner_ref),
                (face_hbm, face_ref),
                (mat_hbm, mat_ref),
                (wall_hbm, wall_ref),
                (cond_hbm, cond_ref),
                (air_hbm, air_even.at[:, pl.ds(1, depth)]),
                (speed_hbm, speed),
                (upwind_hbm, upwind),
            ]
        )
    ]
    for load in loads:
        load.start()
    lax.fori_loop(1, groups, greet, 0)
    for neighbour in (east, west):
        pl.semaphore_signal(barrier, inc=1, device_id={"horiz": neighbour}, device_id_type=MESH)

    plane0 = jnp.zeros((fields, breadth, span), F32)
    for air in airs:
        air[:, 0] = plane0
        air[:, depth + 1] = plane0
    in_z[0] = jnp.zeros((breadth, span), F32)
    result[...] = jnp.zeros_like(result)

    loads[0].wait()
    owned = (lax.broadcasted_iota(I32, (groups, walls), 0) == owner_ref[...]).astype(F32)
    block = 2 * LANES
    blocks = walls // block
    stacked = jnp.concatenate(
        [owned[:, k * block : (k + 1) * block] for k in range(blocks)], axis=0
    )
    lower = (
        lax.broadcasted_iota(I32, (block, block), 0) < lax.broadcasted_iota(I32, (block, block), 1)
    ).astype(F32)
    before = dot(stacked.astype(BF16), lower.astype(BF16))
    totals = jnp.sum(stacked, axis=1, keepdims=True)
    offset = jnp.zeros((groups, 1), F32)
    ranks = []
    for k in range(blocks):
        part = slice(k * groups, (k + 1) * groups)
        ranks.append(
            jnp.sum(stacked[part] * (before[part] + offset), axis=0, keepdims=True)
        )
        offset = offset + totals[part]
    ranks = jnp.concatenate(ranks, axis=1).astype(I32)
    ranks_ref[...] = ranks
    rank_hot[...] = (
        (lax.broadcasted_iota(I32, (cap, walls), 0) == ranks).astype(F32).astype(BF16)
    )

    for load in loads[1:5]:
        load.wait()
    material = mat_ref[...]
    hcoef = jnp.zeros(material.shape, F32)
    for k in range(table_ref.shape[0]):
        hcoef = jnp.where(material == k, table_ref[k], hcoef)
    layer = lax.broadcasted_iota(I32, (ROWS, walls), 0)
    surface = (layer == 0).astype(F32)
    cond8 = jnp.concatenate([cond_ref[...], jnp.zeros((1, walls), F32)], axis=0)
    h_top = surface * hcoef
    p = wall_ref[...]
    e = surface
    values = [face_ref[...].astype(F32), hcoef]
    for step in range(steps):
        values.append(p[0:1])
        if step < steps - 1:
            p = wall_back(p, cond8) - h_top * p
    for _ in range(steps - 2):
        e = wall_back(e, cond8) - h_top * e
        values.append(e[0:1])
    values = jnp.concatenate(values, axis=0)
    for s, piece in enumerate(split(values, 3)):
        for b in range(0, groups, 2):
            pair = jnp.concatenate([piece * owned[b : b + 1], piece * owned[b + 1 : b + 2]], axis=0)
            parts_ref[pl.ds((s * groups + b) * ROWS, 2 * ROWS), :] = pair.astype(BF16)
    placed = dot_nt(parts_ref[...], rank_hot[...])
    n = groups * ROWS
    parcel[...] = placed[:n] + placed[n : 2 * n] + placed[2 * n :]

    def at_rows(k):
        return pl.ds(pl.multiple_of(k * ROWS, ROWS), ROWS)

    def at_lanes(k):
        return pl.ds(pl.multiple_of(lax.rem(k, per_chunk) * cap, cap), cap)

    served[lax.div(me, per_chunk), :, at_lanes(me)] = parcel[at_rows(me), :]

    pl.semaphore_wait(barrier, groups + 1)

    def parcel_copy(d):
        to = lax.rem(me + d, groups)
        return pltpu.make_async_remote_copy(
            src_ref=parcel.at[at_rows(to)],
            dst_ref=served.at[lax.div(me, per_chunk), :, at_lanes(me)],
            send_sem=parcel_send.at[d],
            recv_sem=parcel_recv.at[d],
            device_id={"vert": to},
            device_id_type=MESH,
        )

    def return_copy(d):
        to = lax.rem(me + d, groups)
        return pltpu.make_async_remote_copy(
            src_ref=result.at[lax.div(to, per_chunk), :, at_lanes(to)],
            dst_ref=returned.at[at_rows(me)],
            send_sem=return_send.at[d],
            recv_sem=return_recv.at[d],
            device_id={"vert": to},
            device_id_type=MESH,
        )

    def each(copy, act):
        def body(d, carry):
            act(copy(d))
            return carry

        lax.fori_loop(1, groups, body, 0)

    each(parcel_copy, lambda copy: copy.start())

    def halo_copies(step, air, first, count, group):
        some = pl.ds(first, count)
        return [
            pltpu.make_async_remote_copy(
                src_ref=src,
                dst_ref=dst,
                send_sem=halo_send.at[step, group, k],
                recv_sem=halo_recv.at[step, group, k],
                device_id=to,
                device_id_type=MESH,
            )
            for k, (src, dst, to) in enumerate(
                [
                    (air.at[some, depth], halo_z.at[step, 0, some], {"vert": above}),
                    (air.at[some, 1], halo_z.at[step, 1, some], {"vert": below}),
                    (edge_x.at[step, 1, some], halo_x.at[step, 0, some], {"horiz": east}),
                    (edge_x.at[step, 0, some], halo_x.at[step, 1, some], {"horiz": west}),
                ]
            )
        ]

    pairs = halo_recv.shape[1] - 1
    paired = (fields - 1) // pairs

    def halos_of(step, air, group):
        if isinstance(group, int) and group == pairs:
            return halo_copies(step, air, 0, 1, pairs)
        return halo_copies(step, air, 1 + group * paired, paired, group)

    planes = LANES // breadth

    def split_field(air):
        def body(k, carry):
            block = air[0, pl.ds(1 + k * planes, planes)].reshape(LANES, span).T
            hi = block.astype(BF16)
            field_t[:, pl.ds(pl.multiple_of(k * LANES, LANES), LANES)] = hi
            field_t[:, pl.ds(pl.multiple_of(rows + k * LANES, LANES), LANES)] = (
                block - hi.astype(F32)
            ).astype(BF16)
            return carry

        for k in range(depth // planes):
            body(k, 0)

    loads[5].wait()

    def pack_first(z, carry):
        for f in range(fields):
            edge_x[0, 0, f, pl.ds(z, 1), :] = air_even[f, z + 1, 0:1, :]
            edge_x[0, 1, f, pl.ds(z, 1), :] = air_even[f, z + 1, breadth - 1 : breadth, :]
        return carry

    lax.fori_loop(0, depth, pack_first, 0)
    for group in range(pairs + 1):
        for copy in halos_of(0, air_even, group):
            copy.start()
    split_field(air_even)

    loads[6].wait()
    loads[7].wait()
    row_id = lax.broadcasted_iota(I32, (breadth, span), 0)
    lane_id = lax.broadcasted_iota(I32, (breadth, span), 1)

    def coefficients(z, carry):
        out, inn = [], []
        for d in range(3):
            s = speed[d, z]
            o = s * upwind[d, z].astype(F32)
            out.append(o)
            inn.append(s - o)
            speed[d, z] = o
        in_z[z + 1] = -inn[0]
        in_x_last[pl.ds(z, 1), :] = -inn[1][breadth - 1 : breadth]
        out_x_last[pl.ds(z, 1), :] = out[1][breadth - 1 : breadth]
        low_x = jnp.where(row_id == 0, 0.0, pltpu.roll(-inn[1], 1, 0))
        low_y = jnp.where(lane_id == 0, 0.0, pltpu.roll(-inn[2], 1, 1))
        in_x[z] = low_x
        in_y[z] = low_y
        centre_c[z] = 1.0 - (out[0] + out[1] + out[2]) - (in_z[z] + low_x + low_y)
        return carry

    lax.fori_loop(0, depth, coefficients, 0)
    in_copies = [
        pltpu.make_async_remote_copy(
            src_ref=src,
            dst_ref=dst,
            send_sem=in_send.at[k],
            recv_sem=in_recv.at[k],
            device_id=to,
            device_id_type=MESH,
        )
        for k, (src, dst, to) in enumerate(
            [
                (in_z.at[depth], in_z_halo, {"vert": above}),
                (in_x_last, in_x_halo, {"horiz": east}),
            ]
        )
    ]
    for copy in in_copies:
        copy.start()

    sub8 = lax.broadcasted_iota(I32, (SUBS, LANES), 0)
    lane8 = lax.broadcasted_iota(I32, (SUBS, LANES), 1)

    def stencil(cur, new, z, chosen):
        zero = jnp.zeros((SUBS, LANES), F32)
        first_lane, last_lane = lane8 == 0, lane8 == LANES - 1
        first_sub, last_sub = sub8 == 0, sub8 == SUBS - 1
        for f in chosen:
            kappa = kappa_ref[f]
            tile = {}
            for i in range(x_tiles):
                for h in range(2):
                    tile[i, h] = cur[
                        f, z + 1, SUBS * i : SUBS * (i + 1), LANES * h : LANES * (h + 1)
                    ]
            down = {k: pltpu.roll(t, 1, 0) for k, t in tile.items()}
            up = {k: pltpu.roll(t, SUBS - 1, 0) for k, t in tile.items()}
            for i in range(x_tiles):
                right = [pltpu.roll(tile[i, h], 1, 1) for h in range(2)]
                left = [pltpu.roll(tile[i, h], LANES - 1, 1) for h in range(2)]
                south = [jnp.where(first_lane, 0.0, right[0]), jnp.where(first_lane, *right)]
                north = [
                    jnp.where(last_lane, left[1], left[0]),
                    jnp.where(last_lane, 0.0, left[1]),
                ]
                for h in range(2):
                    at = (slice(SUBS * i, SUBS * (i + 1)), slice(LANES * h, LANES * (h + 1)))
                    m_west = jnp.where(first_sub, down[i - 1, h] if i else zero, down[i, h])
                    m_east = jnp.where(
                        last_sub, up[i + 1, h] if i + 1 < x_tiles else zero, up[i, h]
                    )
                    total = (centre_c[(z,) + at] - 6.0 * kappa) * tile[i, h]
                    total += (speed[(0, z) + at] + kappa) * cur[(f, z + 2) + at]
                    total += (in_z[(z,) + at] + kappa) * cur[(f, z) + at]
                    total += (speed[(1, z) + at] + kappa) * m_east
                    total += (in_x[(z,) + at] + kappa) * m_west
                    total += (speed[(2, z) + at] + kappa) * north[h]
                    total += (in_y[(z,) + at] + kappa) * south[h]
                    new[(f, z + 1) + at] = total

    each(parcel_copy, lambda copy: copy.wait())

    def one_hots(c, carry):
        cell = served[c, 0:1, :].astype(I32)
        hot = (lax.broadcasted_iota(I32, (rows, chunk), 0) == cell // span).astype(F32).astype(BF16)
        row_hot[c, :rows] = hot
        row_hot[c, rows:] = hot
        col_hot[c] = (
            (lax.broadcasted_iota(I32, (span, chunk), 0) == cell % span).astype(F32).astype(BF16)
        )
        return carry

    lax.fori_loop(0, chunks, one_hots, 0)

    def gather(step, c):
        picked = dot(field_t[...], row_hot[c])
        wall = served[c]
        y = wall[0:1].astype(I32) % span
        mask = lax.broadcasted_iota(I32, (span, chunk), 0) == y
        fetched = jnp.sum(jnp.where(mask, picked, 0.0), axis=0, keepdims=True)
        h = wall[1:2]
        half = RATIO * fetched * h
        flow = h * wall[2:3] - half
        flows_ref[pl.ds(c, 1), :] = flow
        result[c, pl.ds(step, 1), :] = flow
        later = [wall[0:1], h, wall[3:4] + half]
        for k in range(1, steps - 1):
            g = steps + 1 + k
            later.append(wall[3 + k : 4 + k] + half * wall[g : g + 1])
        later.append(jnp.zeros_like(h))
        later.append(wall[2 + steps :])
        served[c] = jnp.concatenate(later, axis=0)

    def scatter(c):
        flow = flows_ref[pl.ds(c, 1), :]
        hi = flow.astype(BF16)
        lo = (flow - hi.astype(F32)).astype(BF16)
        hot = col_hot[c]
        where = row_hot[c, :rows]
        added[...] += dot_nt(where, hot * hi) + dot_nt(where, hot * lo)

    def beyond_z(step, cur, new, f):
        kappa = kappa_ref[f]
        beyond = halo_z[step, 0, f] * has_below
        new[f, 1] += kappa * beyond + in_z_halo[...] * (beyond - cur[f, 1])
        beyond = halo_z[step, 1, f] * has_above
        new[f, depth] += (speed[0, depth - 1] + kappa) * beyond
        beyond = halo_x[step, 0, f] * has_west
        fix_x[0, f] = kappa * beyond + in_x_halo[...] * (beyond - edge_x[step, 0, f])
        beyond = halo_x[step, 1, f] * has_east
        fix_x[1, f] = (out_x_last[...] + kappa) * beyond

    def finish(step, cur, new, chosen, walls_too=False):
        for f in chosen:
            beyond_z(step, cur, new, f)

        def body(k, carry):
            for j in range(UNROLL):
                z = k * UNROLL + j
                if walls_too:
                    at = pl.ds(pl.multiple_of(z * breadth, breadth), breadth)
                    new[0, z + 1] += added[at, :]
                for f in chosen:
                    low = new[f, z + 1, 0:1, :] + fix_x[0, f, pl.ds(z, 1), :]
                    high = (
                        new[f, z + 1, breadth - 1 : breadth, :] + fix_x[1, f, pl.ds(z, 1), :]
                    )
                    new[f, z + 1, 0:1, :] = low
                    new[f, z + 1, breadth - 1 : breadth, :] = high
                    edge_x[step + 1, 0, f, pl.ds(z, 1), :] = low
                    edge_x[step + 1, 1, f, pl.ds(z, 1), :] = high
            return carry

        lax.fori_loop(0, depth // UNROLL, body, 0)

    def store(f):
        return pltpu.make_async_copy(
            airs[steps % 2].at[f, pl.ds(1, depth)], air_out.at[f], store_sem.at[f]
        )

    rank_store = pltpu.make_async_copy(ranks_ref, ranks_out, store_sem.at[fields])
    rank_store.start()
    returned_store = pltpu.make_async_copy(returned, returned_out, store_sem.at[fields + 1])

    beside = depth // chunks

    def time_step(step, cur, new):
        last = step == steps - 1

        def body_gather(c, carry):
            gather(step, c)
            for k in range(beside):
                stencil(cur, new, c * beside + k, range(1, fields))
            return carry

        lax.fori_loop(0, chunks, body_gather, 0)

        @pl.when(last)
        def _():
            each(return_copy, lambda copy: copy.start())
            returned[at_rows(me), :] = result[lax.div(me, per_chunk), :, at_lanes(me)]

        @pl.when(step == 0)
        def _():
            for copy in in_copies:
                copy.wait()
            in_z_halo[...] = in_z_halo[...] * has_below
            in_x_halo[...] = in_x_halo[...] * has_west

        for group in range(pairs):
            chosen = [1 + group * paired + k for k in range(paired)]
            for copy in halos_of(step, cur, group):
                copy.wait()
            finish(step, cur, new, chosen)

            @pl.when(last)
            def _():
                for f in chosen:
                    store(f).start()

            @pl.when(jnp.logical_not(last))
            def _():
                for copy in halos_of(step + 1, new, group):
                    copy.start()

        added[...] = jnp.zeros_like(added)

        def body_scatter(c, carry):
            scatter(c)
            for k in range(beside):
                stencil(cur, new, c * beside + k, range(1))
            return carry

        lax.fori_loop(0, chunks, body_scatter, 0)
        for copy in halos_of(step, cur, pairs):
            copy.wait()
        finish(step, cur, new, range(1), True)

        @pl.when(last)
        def _():
            store(0).start()

        @pl.when(jnp.logical_not(last))
        def _():
            for copy in halos_of(step + 1, new, pairs):
                copy.start()
            split_field(new)

    def two_steps(k, carry):
        time_step(2 * k, air_even, air_odd)
        time_step(2 * k + 1, air_odd, air_even)
        return carry

    lax.fori_loop(0, steps // 2, two_steps, 0)
    each(return_copy, lambda copy: copy.wait())
    returned_store.start()
    for copy in [rank_store, returned_store] + [store(f) for f in range(fields)]:
        copy.wait()


def wall_kernel(
    dims,
    air_hbm,
    returned_hbm,
    ranks_hbm,
    owner_hbm,
    wall_hbm,
    cond_hbm,
    saved_hbm,
    air_out,
    wall_out,
    grad_out,
    air,
    returned,
    ranks_ref,
    owner_ref,
    wall_ref,
    cond_ref,
    saved_ref,
    wall_res,
    grad_res,
    load_sem,
    store_sem,
):
    steps, groups = dims
    fields = air.shape[0]
    cap = returned.shape[1]
    walls = wall_ref.shape[1]
    loads = [
        pltpu.make_async_copy(src, dst, load_sem.at[k])
        for k, (src, dst) in enumerate(
            [(air_hbm.at[f], air.at[f]) for f in range(fields)]
            + [
                (ranks_hbm, ranks_ref),
                (owner_hbm, owner_ref),
                (returned_hbm, returned),
                (wall_hbm, wall_ref),
                (cond_hbm, cond_ref),
                (saved_hbm, saved_ref),
            ]
        )
    ]
    for load in loads:
        load.start()
    stores = [
        pltpu.make_async_copy(air.at[f], air_out.at[f], store_sem.at[f]) for f in range(fields)
    ] + [
        pltpu.make_async_copy(wall_res, wall_out, store_sem.at[fields]),
        pltpu.make_async_copy(grad_res, grad_out, store_sem.at[fields + 1]),
    ]
    for f in range(fields):
        loads[f].wait()
        stores[f].start()
    for load in loads[fields:]:
        load.wait()
    rank_hot = (
        (lax.broadcasted_iota(I32, (cap, walls), 0) == ranks_ref[...]).astype(F32).astype(BF16)
    )
    owned = (lax.broadcasted_iota(I32, (groups, walls), 0) == owner_ref[...]).astype(F32)
    placed = dot(jnp.concatenate(split(returned[...], 3), axis=0).astype(BF16), rank_hot)
    n = groups * ROWS
    placed = placed[:n] + placed[n : 2 * n] + placed[2 * n :]
    flows = jnp.zeros((ROWS, walls), F32)
    for b in range(groups):
        flows = flows + owned[b : b + 1] * placed[b * ROWS : (b + 1) * ROWS]
    surface = (lax.broadcasted_iota(I32, (ROWS, walls), 0) == 0).astype(F32)
    p = wall_ref[...]
    cond8 = jnp.concatenate([cond_ref[...], jnp.zeros((1, walls), F32)], axis=0)
    grad = jnp.zeros((ROWS, walls), F32)
    for step in range(steps):
        saved = saved_ref[steps - 1 - step]
        grad = grad - (pltpu.roll(saved, ROWS - 1, 0) - saved) * (pltpu.roll(p, ROWS - 1, 0) - p)
        p = wall_back(p, cond8) - surface * flows[step : step + 1]
    wall_res[...] = p
    grad_res[...] = grad[: ROWS - 1]
    for copy in stores[fields:]:
        copy.start()
    for copy in stores:
        copy.wait()


def per_device(
    air_seed,
    wall_seed,
    speed,
    upwind,
    diffusivity,
    conductivity,
    wall_saved,
    heat_table,
    interface,
    owner,
    material,
):
    groups, columns = lax.axis_size("vert"), lax.axis_size("horiz")
    steps = wall_saved.shape[0]
    walls = interface.shape[0]
    cap = walls // 4
    fields, depth, breadth, span = air_seed.shape
    rows = depth * breadth
    chunks = 2
    pairs = 1
    chunk = groups * cap // chunks
    smem = pl.BlockSpec(memory_space=pltpu.SMEM)
    hbm = pl.BlockSpec(memory_space=pl.ANY)
    dma = pltpu.SemaphoreType.DMA
    plane = (breadth, span)
    brick = (depth, breadth, span)
    side = (depth, span)
    scratch = [
        pltpu.VMEM(wall_seed.shape, F32),
        pltpu.VMEM(conductivity.shape, F32),
        pltpu.VMEM((1, walls), I32),
        pltpu.VMEM((1, walls), I32),
        pltpu.VMEM((1, walls), I32),
        pltpu.VMEM((fields, depth + 2) + plane, F32),
        pltpu.VMEM((fields, depth + 2) + plane, F32),
        pltpu.VMEM((3,) + brick, F32),
        pltpu.VMEM((3,) + brick, I32),
        pltpu.VMEM((depth + 1,) + plane, F32),
        pltpu.VMEM(brick, F32),
        pltpu.VMEM(brick, F32),
        pltpu.VMEM(brick, F32),
        pltpu.VMEM(side, F32),
        pltpu.VMEM(side, F32),
        pltpu.VMEM(plane, F32),
        pltpu.VMEM(side, F32),
        pltpu.VMEM((steps, 2, fields) + plane, F32),
        pltpu.VMEM((steps, 2, fields) + side, F32),
        pltpu.VMEM((steps + 1, 2, fields) + side, F32),
        pltpu.VMEM((2, fields) + side, F32),
        pltpu.VMEM((span, 2 * rows), BF16),
        pltpu.VMEM((chunks, 2 * rows, chunk), BF16),
        pltpu.VMEM((chunks, span, chunk), BF16),
        pltpu.VMEM((chunks, chunk), F32),
        pltpu.VMEM((rows, span), F32),
        pltpu.VMEM((3 * groups * ROWS, walls), BF16),
        pltpu.VMEM((cap, walls), BF16),
        pltpu.VMEM((1, walls), I32),
        pltpu.VMEM((groups * ROWS, cap), F32),
        pltpu.VMEM((chunks, ROWS, chunk), F32),
        pltpu.VMEM((chunks, ROWS, chunk), F32),
        pltpu.VMEM((groups * ROWS, cap), F32),
        dma((8,)),
        dma((fields + 2,)),
        dma((2,)),
        dma((2,)),
        dma((steps, pairs + 1, 4)),
        dma((steps, pairs + 1, 4)),
        dma((groups,)),
        dma((groups,)),
        dma((groups,)),
        dma((groups,)),
    ]
    owners = owner.reshape(1, walls)
    air, returned, ranks = pl.pallas_call(
        functools.partial(kernel, (steps, groups, columns)),
        out_shape=(
            jax.ShapeDtypeStruct(air_seed.shape, F32),
            jax.ShapeDtypeStruct((groups * ROWS, cap), F32),
            jax.ShapeDtypeStruct((1, walls), I32),
        ),
        in_specs=[smem, smem] + [hbm] * 8,
        out_specs=(hbm, hbm, hbm),
        scratch_shapes=scratch,
        compiler_params=pltpu.CompilerParams(
            collective_id=0, has_side_effects=True, vmem_limit_bytes=VMEM_BYTES
        ),
        cost_estimate=pl.CostEstimate(
            flops=2 * steps * 4 * groups * cap * rows * span,
            bytes_accessed=40 * rows * span,
            transcendentals=0,
        ),
    )(
        diffusivity,
        heat_table,
        wall_seed,
        conductivity,
        interface.reshape(1, walls),
        owners,
        material.reshape(1, walls),
        air_seed,
        speed,
        upwind,
    )
    return pl.pallas_call(
        functools.partial(wall_kernel, (steps, groups)),
        out_shape=(
            jax.ShapeDtypeStruct(air_seed.shape, F32),
            jax.ShapeDtypeStruct(wall_seed.shape, F32),
            jax.ShapeDtypeStruct(conductivity.shape, F32),
        ),
        in_specs=[hbm] * 7,
        out_specs=(hbm, hbm, hbm),
        scratch_shapes=[
            pltpu.VMEM(air_seed.shape, F32),
            pltpu.VMEM((groups * ROWS, cap), F32),
            pltpu.VMEM((1, walls), I32),
            pltpu.VMEM((1, walls), I32),
            pltpu.VMEM(wall_seed.shape, F32),
            pltpu.VMEM(conductivity.shape, F32),
            pltpu.VMEM(wall_saved.shape, F32),
            pltpu.VMEM(wall_seed.shape, F32),
            pltpu.VMEM(conductivity.shape, F32),
            dma((6 + fields,)),
            dma((2 + fields,)),
        ],
        compiler_params=pltpu.CompilerParams(vmem_limit_bytes=VMEM_BYTES),
        cost_estimate=pl.CostEstimate(
            flops=2 * 3 * groups * ROWS * cap * walls,
            bytes_accessed=48 * rows * span,
            transcendentals=0,
        ),
    )(air, returned, ranks, owners, wall_seed, conductivity, wall_saved)


def solution(mesh):
    air = P(None, "vert", "horiz", None)
    wall = P(None, ("horiz", "vert"))
    column = P(("horiz", "vert"))
    return jax.shard_map(
        per_device,
        mesh=mesh,
        in_specs=(
            air,
            wall,
            air,
            air,
            P(),
            wall,
            P(None, None, ("horiz", "vert")),
            P(),
            column,
            P(("horiz", "vert"), None),
            column,
        ),
        out_specs=(air, wall, wall),
        check_vma=False,
    )
```

```python
import functools

import jax
import jax.numpy as jnp
from jax import lax
from jax.experimental import pallas as pl
from jax.experimental.pallas import tpu as pltpu
from jax.sharding import PartitionSpec as P

F32, BF16, I32 = jnp.float32, jnp.bfloat16, jnp.int32
MESH = pl.DeviceIdType.MESH
LANES, SUBS = 128, 8
RATIO = 0.5
UNROLL = 2
VMEM_BYTES = 64 * 1024 * 1024 - 64 * 1024
ROWS = 8
NT = (((1,), (1,)), ((), ()))


def dot(a, b):
    return jnp.dot(a, b, preferred_element_type=F32)


def dot_nt(a, b):
    return lax.dot_general(a, b, NT, preferred_element_type=F32)


def split(value, parts):
    pieces = []
    for _ in range(parts):
        piece = value.astype(BF16).astype(F32)
        pieces.append(piece)
        value = value - piece
    return pieces


def wall_back(p, cond8):
    flux = cond8 * (pltpu.roll(p, ROWS - 1, 0) - p)
    return p + flux - pltpu.roll(flux, 1, 0)


def kernel(
    dims,
    kappa_ref,
    table_ref,
    wall_hbm,
    cond_hbm,
    face_hbm,
    owner_hbm,
    mat_hbm,
    air_hbm,
    speed_hbm,
    upwind_hbm,
    air_out,
    returned_out,
    ranks_out,
    wall_ref,
    cond_ref,
    face_ref,
    owner_ref,
    mat_ref,
    air_even,
    air_odd,
    speed,
    upwind,
    in_z,
    in_x,
    in_y,
    centre_c,
    out_x_last,
    in_x_last,
    in_z_halo,
    in_x_halo,
    halo_z,
    halo_x,
    edge_x,
    fix_x,
    field_t,
    row_hot,
    col_hot,
    flows_ref,
    added,
    parts_ref,
    rank_hot,
    ranks_ref,
    parcel,
    served,
    result,
    returned,
    load_sem,
    store_sem,
    in_send,
    in_recv,
    halo_send,
    halo_recv,
    parcel_send,
    parcel_recv,
    return_send,
    return_recv,
):
    steps, groups, columns = dims
    airs = (air_even, air_odd)
    fields, depth, breadth, span = air_out.shape
    walls = face_ref.shape[1]
    cap = rank_hot.shape[0]
    rows = depth * breadth
    x_tiles = breadth // SUBS
    chunks, _, chunk = served.shape
    per_chunk = chunk // cap
    me = lax.axis_index("vert")
    col = lax.axis_index("horiz")
    above, below = lax.rem(me + 1, groups), lax.rem(me + groups - 1, groups)
    east, west = lax.rem(col + 1, columns), lax.rem(col + columns - 1, columns)
    has_below = jnp.where(me > 0, 1.0, 0.0).astype(F32)
    has_above = jnp.where(me < groups - 1, 1.0, 0.0).astype(F32)
    has_west = jnp.where(col > 0, 1.0, 0.0).astype(F32)
    has_east = jnp.where(col < columns - 1, 1.0, 0.0).astype(F32)

    barrier = pltpu.get_barrier_semaphore()

    def greet(d, carry):
        pl.semaphore_signal(
            barrier, inc=1, device_id={"vert": lax.rem(me + d, groups)}, device_id_type=MESH
        )
        return carry

    loads = [
        pltpu.make_async_copy(src, dst, load_sem.at[k])
        for k, (src, dst) in enumerate(
            [
                (owner_hbm, owner_ref),
                (face_hbm, face_ref),
                (mat_hbm, mat_ref),
                (wall_hbm, wall_ref),
                (cond_hbm, cond_ref),
                (air_hbm, air_even.at[:, pl.ds(1, depth)]),
                (speed_hbm, speed),
                (upwind_hbm, upwind),
            ]
        )
    ]
    for load in loads:
        load.start()
    lax.fori_loop(1, groups, greet, 0)
    for neighbour in (east, west):
        pl.semaphore_signal(barrier, inc=1, device_id={"horiz": neighbour}, device_id_type=MESH)

    plane0 = jnp.zeros((fields, breadth, span), F32)
    for air in airs:
        air[:, 0] = plane0
        air[:, depth + 1] = plane0
    in_z[0] = jnp.zeros((breadth, span), F32)
    result[...] = jnp.zeros_like(result)

    loads[0].wait()
    owned = (lax.broadcasted_iota(I32, (groups, walls), 0) == owner_ref[...]).astype(F32)
    block = 2 * LANES
    blocks = walls // block
    stacked = jnp.concatenate(
        [owned[:, k * block : (k + 1) * block] for k in range(blocks)], axis=0
    )
    lower = (
        lax.broadcasted_iota(I32, (block, block), 0) < lax.broadcasted_iota(I32, (block, block), 1)
    ).astype(F32)
    before = dot(stacked.astype(BF16), lower.astype(BF16))
    totals = jnp.sum(stacked, axis=1, keepdims=True)
    offset = jnp.zeros((groups, 1), F32)
    ranks = []
    for k in range(blocks):
        part = slice(k * groups, (k + 1) * groups)
        ranks.append(
            jnp.sum(stacked[part] * (before[part] + offset), axis=0, keepdims=True)
        )
        offset = offset + totals[part]
    ranks = jnp.concatenate(ranks, axis=1).astype(I32)
    ranks_ref[...] = ranks
    rank_hot[...] = (
        (lax.broadcasted_iota(I32, (cap, walls), 0) == ranks).astype(F32).astype(BF16)
    )

    for load in loads[1:5]:
        load.wait()
    material = mat_ref[...]
    hcoef = jnp.zeros(material.shape, F32)
    for k in range(table_ref.shape[0]):
        hcoef = jnp.where(material == k, table_ref[k], hcoef)
    layer = lax.broadcasted_iota(I32, (ROWS, walls), 0)
    surface = (layer == 0).astype(F32)
    cond8 = jnp.concatenate([cond_ref[...], jnp.zeros((1, walls), F32)], axis=0)
    h_top = surface * hcoef
    p = wall_ref[...]
    e = surface
    values = [face_ref[...].astype(F32), hcoef]
    for step in range(steps):
        values.append(p[0:1])
        if step < steps - 1:
            p = wall_back(p, cond8) - h_top * p
    for _ in range(steps - 2):
        e = wall_back(e, cond8) - h_top * e
        values.append(e[0:1])
    values = jnp.concatenate(values, axis=0)
    for s, piece in enumerate(split(values, 3)):
        for b in range(0, groups, 2):
            pair = jnp.concatenate([piece * owned[b : b + 1], piece * owned[b + 1 : b + 2]], axis=0)
            parts_ref[pl.ds((s * groups + b) * ROWS, 2 * ROWS), :] = pair.astype(BF16)
    placed = dot_nt(parts_ref[...], rank_hot[...])
    n = groups * ROWS
    parcel[...] = placed[:n] + placed[n : 2 * n] + placed[2 * n :]

    def at_rows(k):
        return pl.ds(pl.multiple_of(k * ROWS, ROWS), ROWS)

    def at_lanes(k):
        return pl.ds(pl.multiple_of(lax.rem(k, per_chunk) * cap, cap), cap)

    served[lax.div(me, per_chunk), :, at_lanes(me)] = parcel[at_rows(me), :]

    pl.semaphore_wait(barrier, groups + 1)

    def parcel_copy(d):
        to = lax.rem(me + d, groups)
        return pltpu.make_async_remote_copy(
            src_ref=parcel.at[at_rows(to)],
            dst_ref=served.at[lax.div(me, per_chunk), :, at_lanes(me)],
            send_sem=parcel_send.at[d],
            recv_sem=parcel_recv.at[d],
            device_id={"vert": to},
            device_id_type=MESH,
        )

    def return_copy(d):
        to = lax.rem(me + d, groups)
        return pltpu.make_async_remote_copy(
            src_ref=result.at[lax.div(to, per_chunk), :, at_lanes(to)],
            dst_ref=returned.at[at_rows(me)],
            send_sem=return_send.at[d],
            recv_sem=return_recv.at[d],
            device_id={"vert": to},
            device_id_type=MESH,
        )

    def each(copy, act):
        def body(d, carry):
            act(copy(d))
            return carry

        lax.fori_loop(1, groups, body, 0)

    each(parcel_copy, lambda copy: copy.start())

    def halo_copies(step, air, first, count, group):
        some = pl.ds(first, count)
        return [
            pltpu.make_async_remote_copy(
                src_ref=src,
                dst_ref=dst,
                send_sem=halo_send.at[step, group, k],
                recv_sem=halo_recv.at[step, group, k],
                device_id=to,
                device_id_type=MESH,
            )
            for k, (src, dst, to) in enumerate(
                [
                    (air.at[some, depth], halo_z.at[step, 0, some], {"vert": above}),
                    (air.at[some, 1], halo_z.at[step, 1, some], {"vert": below}),
                    (edge_x.at[step, 1, some], halo_x.at[step, 0, some], {"horiz": east}),
                    (edge_x.at[step, 0, some], halo_x.at[step, 1, some], {"horiz": west}),
                ]
            )
        ]

    pairs = halo_recv.shape[1] - 1
    paired = (fields - 1) // pairs

    def halos_of(step, air, group):
        if isinstance(group, int) and group == pairs:
            return halo_copies(step, air, 0, 1, pairs)
        return halo_copies(step, air, 1 + group * paired, paired, group)

    planes = LANES // breadth

    def split_field(air):
        def body(k, carry):
            block = air[0, pl.ds(1 + k * planes, planes)].reshape(LANES, span).T
            hi = block.astype(BF16)
            field_t[:, pl.ds(pl.multiple_of(k * LANES, LANES), LANES)] = hi
            field_t[:, pl.ds(pl.multiple_of(rows + k * LANES, LANES), LANES)] = (
                block - hi.astype(F32)
            ).astype(BF16)
            return carry

        for k in range(depth // planes):
            body(k, 0)

    loads[5].wait()

    def pack_first(z, carry):
        for f in range(fields):
            edge_x[0, 0, f, pl.ds(z, 1), :] = air_even[f, z + 1, 0:1, :]
            edge_x[0, 1, f, pl.ds(z, 1), :] = air_even[f, z + 1, breadth - 1 : breadth, :]
        return carry

    lax.fori_loop(0, depth, pack_first, 0)
    for group in range(pairs + 1):
        for copy in halos_of(0, air_even, group):
            copy.start()
    split_field(air_even)

    loads[6].wait()
    loads[7].wait()
    row_id = lax.broadcasted_iota(I32, (breadth, span), 0)
    lane_id = lax.broadcasted_iota(I32, (breadth, span), 1)

    def coefficients(z, carry):
        out, inn = [], []
        for d in range(3):
            s = speed[d, z]
            o = s * upwind[d, z].astype(F32)
            out.append(o)
            inn.append(s - o)
            speed[d, z] = o
        in_z[z + 1] = -inn[0]
        in_x_last[pl.ds(z, 1), :] = -inn[1][breadth - 1 : breadth]
        out_x_last[pl.ds(z, 1), :] = out[1][breadth - 1 : breadth]
        low_x = jnp.where(row_id == 0, 0.0, pltpu.roll(-inn[1], 1, 0))
        low_y = jnp.where(lane_id == 0, 0.0, pltpu.roll(-inn[2], 1, 1))
        in_x[z] = low_x
        in_y[z] = low_y
        centre_c[z] = 1.0 - (out[0] + out[1] + out[2]) - (in_z[z] + low_x + low_y)
        return carry

    lax.fori_loop(0, depth, coefficients, 0)
    in_copies = [
        pltpu.make_async_remote_copy(
            src_ref=src,
            dst_ref=dst,
            send_sem=in_send.at[k],
            recv_sem=in_recv.at[k],
            device_id=to,
            device_id_type=MESH,
        )
        for k, (src, dst, to) in enumerate(
            [
                (in_z.at[depth], in_z_halo, {"vert": above}),
                (in_x_last, in_x_halo, {"horiz": east}),
            ]
        )
    ]
    for copy in in_copies:
        copy.start()

    sub8 = lax.broadcasted_iota(I32, (SUBS, LANES), 0)
    lane8 = lax.broadcasted_iota(I32, (SUBS, LANES), 1)

    def stencil(cur, new, z, chosen):
        zero = jnp.zeros((SUBS, LANES), F32)
        first_lane, last_lane = lane8 == 0, lane8 == LANES - 1
        first_sub, last_sub = sub8 == 0, sub8 == SUBS - 1
        for f in chosen:
            kappa = kappa_ref[f]
            tile = {}
            for i in range(x_tiles):
                for h in range(2):
                    tile[i, h] = cur[
                        f, z + 1, SUBS * i : SUBS * (i + 1), LANES * h : LANES * (h + 1)
                    ]
            down = {k: pltpu.roll(t, 1, 0) for k, t in tile.items()}
            up = {k: pltpu.roll(t, SUBS - 1, 0) for k, t in tile.items()}
            for i in range(x_tiles):
                right = [pltpu.roll(tile[i, h], 1, 1) for h in range(2)]
                left = [pltpu.roll(tile[i, h], LANES - 1, 1) for h in range(2)]
                south = [jnp.where(first_lane, 0.0, right[0]), jnp.where(first_lane, *right)]
                north = [
                    jnp.where(last_lane, left[1], left[0]),
                    jnp.where(last_lane, 0.0, left[1]),
                ]
                for h in range(2):
                    at = (slice(SUBS * i, SUBS * (i + 1)), slice(LANES * h, LANES * (h + 1)))
                    m_west = jnp.where(first_sub, down[i - 1, h] if i else zero, down[i, h])
                    m_east = jnp.where(
                        last_sub, up[i + 1, h] if i + 1 < x_tiles else zero, up[i, h]
                    )
                    total = (centre_c[(z,) + at] - 6.0 * kappa) * tile[i, h]
                    total += (speed[(0, z) + at] + kappa) * cur[(f, z + 2) + at]
                    total += (in_z[(z,) + at] + kappa) * cur[(f, z) + at]
                    total += (speed[(1, z) + at] + kappa) * m_east
                    total += (in_x[(z,) + at] + kappa) * m_west
                    total += (speed[(2, z) + at] + kappa) * north[h]
                    total += (in_y[(z,) + at] + kappa) * south[h]
                    new[(f, z + 1) + at] = total

    def stencil_first(z, carry):
        stencil(air_even, air_odd, z, range(1, fields))
        return carry

    lax.fori_loop(0, depth, stencil_first, 0)
    each(parcel_copy, lambda copy: copy.wait())

    def one_hots(c, carry):
        cell = served[c, 0:1, :].astype(I32)
        hot = (lax.broadcasted_iota(I32, (rows, chunk), 0) == cell // span).astype(F32).astype(BF16)
        row_hot[c, :rows] = hot
        row_hot[c, rows:] = hot
        col_hot[c] = (
            (lax.broadcasted_iota(I32, (span, chunk), 0) == cell % span).astype(F32).astype(BF16)
        )
        return carry

    lax.fori_loop(0, chunks, one_hots, 0)

    def gather(step, c):
        picked = dot(field_t[...], row_hot[c])
        wall = served[c]
        y = wall[0:1].astype(I32) % span
        mask = lax.broadcasted_iota(I32, (span, chunk), 0) == y
        fetched = jnp.sum(jnp.where(mask, picked, 0.0), axis=0, keepdims=True)
        h = wall[1:2]
        half = RATIO * fetched * h
        flow = h * wall[2:3] - half
        flows_ref[pl.ds(c, 1), :] = flow
        result[c, pl.ds(step, 1), :] = flow
        later = [wall[0:1], h, wall[3:4] + half]
        for k in range(1, steps - 1):
            g = steps + 1 + k
            later.append(wall[3 + k : 4 + k] + half * wall[g : g + 1])
        later.append(jnp.zeros_like(h))
        later.append(wall[2 + steps :])
        served[c] = jnp.concatenate(later, axis=0)

    def scatter(c):
        flow = flows_ref[pl.ds(c, 1), :]
        hi = flow.astype(BF16)
        lo = (flow - hi.astype(F32)).astype(BF16)
        hot = col_hot[c]
        where = row_hot[c, :rows]
        added[...] += dot_nt(where, hot * hi) + dot_nt(where, hot * lo)

    def beyond_z(step, cur, new, f):
        kappa = kappa_ref[f]
        beyond = halo_z[step, 0, f] * has_below
        new[f, 1] += kappa * beyond + in_z_halo[...] * (beyond - cur[f, 1])
        beyond = halo_z[step, 1, f] * has_above
        new[f, depth] += (speed[0, depth - 1] + kappa) * beyond
        beyond = halo_x[step, 0, f] * has_west
        fix_x[0, f] = kappa * beyond + in_x_halo[...] * (beyond - edge_x[step, 0, f])
        beyond = halo_x[step, 1, f] * has_east
        fix_x[1, f] = (out_x_last[...] + kappa) * beyond

    def finish(step, cur, new, chosen, walls_too=False):
        for f in chosen:
            beyond_z(step, cur, new, f)

        def body(k, carry):
            for j in range(UNROLL):
                z = k * UNROLL + j
                if walls_too:
                    at = pl.ds(pl.multiple_of(z * breadth, breadth), breadth)
                    new[0, z + 1] += added[at, :]
                for f in chosen:
                    low = new[f, z + 1, 0:1, :] + fix_x[0, f, pl.ds(z, 1), :]
                    high = (
                        new[f, z + 1, breadth - 1 : breadth, :] + fix_x[1, f, pl.ds(z, 1), :]
                    )
                    new[f, z + 1, 0:1, :] = low
                    new[f, z + 1, breadth - 1 : breadth, :] = high
                    edge_x[step + 1, 0, f, pl.ds(z, 1), :] = low
                    edge_x[step + 1, 1, f, pl.ds(z, 1), :] = high
            return carry

        lax.fori_loop(0, depth // UNROLL, body, 0)

    def store(f):
        return pltpu.make_async_copy(
            airs[steps % 2].at[f, pl.ds(1, depth)], air_out.at[f], store_sem.at[f]
        )

    rank_store = pltpu.make_async_copy(ranks_ref, ranks_out, store_sem.at[fields])
    rank_store.start()
    returned_store = pltpu.make_async_copy(returned, returned_out, store_sem.at[fields + 1])

    beside = depth // chunks

    def time_step(step, cur, new):
        last = step == steps - 1

        def body_gather(c, carry):
            @pl.when(step == 0)
            def _():
                gather(step, c)

            @pl.when(step > 0)
            def _():
                gather(step, c)
                for k in range(beside):
                    stencil(cur, new, c * beside + k, range(1, fields))

            @pl.when(last)
            def _():
                def send_back(k, carry):
                    d = lax.rem(c * per_chunk + k - me + groups, groups)

                    @pl.when(d > 0)
                    def _():
                        return_copy(d).start()

                    return carry

                lax.fori_loop(0, per_chunk, send_back, 0)

            return carry

        lax.fori_loop(0, chunks, body_gather, 0)

        @pl.when(last)
        def _():
            returned[at_rows(me), :] = result[lax.div(me, per_chunk), :, at_lanes(me)]

        @pl.when(step == 0)
        def _():
            for copy in in_copies:
                copy.wait()
            in_z_halo[...] = in_z_halo[...] * has_below
            in_x_halo[...] = in_x_halo[...] * has_west

        for group in range(pairs):
            chosen = [1 + group * paired + k for k in range(paired)]
            for copy in halos_of(step, cur, group):
                copy.wait()
            finish(step, cur, new, chosen)

            @pl.when(last)
            def _():
                for f in chosen:
                    store(f).start()

            @pl.when(jnp.logical_not(last))
            def _():
                for copy in halos_of(step + 1, new, group):
                    copy.start()

        added[...] = jnp.zeros_like(added)

        def body_scatter(c, carry):
            scatter(c)
            for k in range(beside):
                stencil(cur, new, c * beside + k, range(1))
            return carry

        lax.fori_loop(0, chunks, body_scatter, 0)
        for copy in halos_of(step, cur, pairs):
            copy.wait()
        finish(step, cur, new, range(1), True)

        @pl.when(last)
        def _():
            store(0).start()

        @pl.when(jnp.logical_not(last))
        def _():
            for copy in halos_of(step + 1, new, pairs):
                copy.start()
            split_field(new)

    def two_steps(k, carry):
        time_step(2 * k, air_even, air_odd)
        time_step(2 * k + 1, air_odd, air_even)
        return carry

    lax.fori_loop(0, steps // 2, two_steps, 0)
    each(return_copy, lambda copy: copy.wait())
    returned_store.start()
    for copy in [rank_store, returned_store] + [store(f) for f in range(fields)]:
        copy.wait()


def wall_kernel(
    dims,
    air_hbm,
    returned_hbm,
    ranks_hbm,
    owner_hbm,
    wall_hbm,
    cond_hbm,
    saved_hbm,
    air_out,
    wall_out,
    grad_out,
    air,
    returned,
    ranks_ref,
    owner_ref,
    wall_ref,
    cond_ref,
    saved_ref,
    wall_res,
    grad_res,
    load_sem,
    store_sem,
):
    steps, groups = dims
    fields = air.shape[0]
    cap = returned.shape[1]
    walls = wall_ref.shape[1]
    loads = [
        pltpu.make_async_copy(src, dst, load_sem.at[k])
        for k, (src, dst) in enumerate(
            [(air_hbm.at[f], air.at[f]) for f in range(fields)]
            + [
                (ranks_hbm, ranks_ref),
                (owner_hbm, owner_ref),
                (returned_hbm, returned),
                (wall_hbm, wall_ref),
                (cond_hbm, cond_ref),
                (saved_hbm, saved_ref),
            ]
        )
    ]
    for load in loads:
        load.start()
    stores = [
        pltpu.make_async_copy(air.at[f], air_out.at[f], store_sem.at[f]) for f in range(fields)
    ] + [
        pltpu.make_async_copy(wall_res, wall_out, store_sem.at[fields]),
        pltpu.make_async_copy(grad_res, grad_out, store_sem.at[fields + 1]),
    ]
    for f in range(fields):
        loads[f].wait()
        stores[f].start()
    for load in loads[fields:]:
        load.wait()
    rank_hot = (
        (lax.broadcasted_iota(I32, (cap, walls), 0) == ranks_ref[...]).astype(F32).astype(BF16)
    )
    owned = (lax.broadcasted_iota(I32, (groups, walls), 0) == owner_ref[...]).astype(F32)
    placed = dot(jnp.concatenate(split(returned[...], 3), axis=0).astype(BF16), rank_hot)
    n = groups * ROWS
    placed = placed[:n] + placed[n : 2 * n] + placed[2 * n :]
    flows = jnp.zeros((ROWS, walls), F32)
    for b in range(groups):
        flows = flows + owned[b : b + 1] * placed[b * ROWS : (b + 1) * ROWS]
    surface = (lax.broadcasted_iota(I32, (ROWS, walls), 0) == 0).astype(F32)
    p = wall_ref[...]
    cond8 = jnp.concatenate([cond_ref[...], jnp.zeros((1, walls), F32)], axis=0)
    grad = jnp.zeros((ROWS, walls), F32)
    for step in range(steps):
        saved = saved_ref[steps - 1 - step]
        grad = grad - (pltpu.roll(saved, ROWS - 1, 0) - saved) * (pltpu.roll(p, ROWS - 1, 0) - p)
        p = wall_back(p, cond8) - surface * flows[step : step + 1]
    wall_res[...] = p
    grad_res[...] = grad[: ROWS - 1]
    for copy in stores[fields:]:
        copy.start()
    for copy in stores:
        copy.wait()


def per_device(
    air_seed,
    wall_seed,
    speed,
    upwind,
    diffusivity,
    conductivity,
    wall_saved,
    heat_table,
    interface,
    owner,
    material,
):
    groups, columns = lax.axis_size("vert"), lax.axis_size("horiz")
    steps = wall_saved.shape[0]
    walls = interface.shape[0]
    cap = walls // 4
    fields, depth, breadth, span = air_seed.shape
    rows = depth * breadth
    chunks = 2
    pairs = 1
    chunk = groups * cap // chunks
    smem = pl.BlockSpec(memory_space=pltpu.SMEM)
    hbm = pl.BlockSpec(memory_space=pl.ANY)
    dma = pltpu.SemaphoreType.DMA
    plane = (breadth, span)
    brick = (depth, breadth, span)
    side = (depth, span)
    scratch = [
        pltpu.VMEM(wall_seed.shape, F32),
        pltpu.VMEM(conductivity.shape, F32),
        pltpu.VMEM((1, walls), I32),
        pltpu.VMEM((1, walls), I32),
        pltpu.VMEM((1, walls), I32),
        pltpu.VMEM((fields, depth + 2) + plane, F32),
        pltpu.VMEM((fields, depth + 2) + plane, F32),
        pltpu.VMEM((3,) + brick, F32),
        pltpu.VMEM((3,) + brick, I32),
        pltpu.VMEM((depth + 1,) + plane, F32),
        pltpu.VMEM(brick, F32),
        pltpu.VMEM(brick, F32),
        pltpu.VMEM(brick, F32),
        pltpu.VMEM(side, F32),
        pltpu.VMEM(side, F32),
        pltpu.VMEM(plane, F32),
        pltpu.VMEM(side, F32),
        pltpu.VMEM((steps, 2, fields) + plane, F32),
        pltpu.VMEM((steps, 2, fields) + side, F32),
        pltpu.VMEM((steps + 1, 2, fields) + side, F32),
        pltpu.VMEM((2, fields) + side, F32),
        pltpu.VMEM((span, 2 * rows), BF16),
        pltpu.VMEM((chunks, 2 * rows, chunk), BF16),
        pltpu.VMEM((chunks, span, chunk), BF16),
        pltpu.VMEM((chunks, chunk), F32),
        pltpu.VMEM((rows, span), F32),
        pltpu.VMEM((3 * groups * ROWS, walls), BF16),
        pltpu.VMEM((cap, walls), BF16),
        pltpu.VMEM((1, walls), I32),
        pltpu.VMEM((groups * ROWS, cap), F32),
        pltpu.VMEM((chunks, ROWS, chunk), F32),
        pltpu.VMEM((chunks, ROWS, chunk), F32),
        pltpu.VMEM((groups * ROWS, cap), F32),
        dma((8,)),
        dma((fields + 2,)),
        dma((2,)),
        dma((2,)),
        dma((steps, pairs + 1, 4)),
        dma((steps, pairs + 1, 4)),
        dma((groups,)),
        dma((groups,)),
        dma((groups,)),
        dma((groups,)),
    ]
    owners = owner.reshape(1, walls)
    air, returned, ranks = pl.pallas_call(
        functools.partial(kernel, (steps, groups, columns)),
        out_shape=(
            jax.ShapeDtypeStruct(air_seed.shape, F32),
            jax.ShapeDtypeStruct((groups * ROWS, cap), F32),
            jax.ShapeDtypeStruct((1, walls), I32),
        ),
        in_specs=[smem, smem] + [hbm] * 8,
        out_specs=(hbm, hbm, hbm),
        scratch_shapes=scratch,
        compiler_params=pltpu.CompilerParams(
            collective_id=0, has_side_effects=True, vmem_limit_bytes=VMEM_BYTES
        ),
        cost_estimate=pl.CostEstimate(
            flops=2 * steps * 4 * groups * cap * rows * span,
            bytes_accessed=40 * rows * span,
            transcendentals=0,
        ),
    )(
        diffusivity,
        heat_table,
        wall_seed,
        conductivity,
        interface.reshape(1, walls),
        owners,
        material.reshape(1, walls),
        air_seed,
        speed,
        upwind,
    )
    return pl.pallas_call(
        functools.partial(wall_kernel, (steps, groups)),
        out_shape=(
            jax.ShapeDtypeStruct(air_seed.shape, F32),
            jax.ShapeDtypeStruct(wall_seed.shape, F32),
            jax.ShapeDtypeStruct(conductivity.shape, F32),
        ),
        in_specs=[hbm] * 7,
        out_specs=(hbm, hbm, hbm),
        scratch_shapes=[
            pltpu.VMEM(air_seed.shape, F32),
            pltpu.VMEM((groups * ROWS, cap), F32),
            pltpu.VMEM((1, walls), I32),
            pltpu.VMEM((1, walls), I32),
            pltpu.VMEM(wall_seed.shape, F32),
            pltpu.VMEM(conductivity.shape, F32),
            pltpu.VMEM(wall_saved.shape, F32),
            pltpu.VMEM(wall_seed.shape, F32),
            pltpu.VMEM(conductivity.shape, F32),
            dma((6 + fields,)),
            dma((2 + fields,)),
        ],
        compiler_params=pltpu.CompilerParams(vmem_limit_bytes=VMEM_BYTES),
        cost_estimate=pl.CostEstimate(
            flops=2 * 3 * groups * ROWS * cap * walls,
            bytes_accessed=48 * rows * span,
            transcendentals=0,
        ),
    )(air, returned, ranks, owners, wall_seed, conductivity, wall_saved)


def solution(mesh):
    air = P(None, "vert", "horiz", None)
    wall = P(None, ("horiz", "vert"))
    column = P(("horiz", "vert"))
    return jax.shard_map(
        per_device,
        mesh=mesh,
        in_specs=(
            air,
            wall,
            air,
            air,
            P(),
            wall,
            P(None, None, ("horiz", "vert")),
            P(),
            column,
            P(("horiz", "vert"), None),
            column,
        ),
        out_specs=(air, wall, wall),
        check_vma=False,
    )
```

```python
import functools

import jax
import jax.numpy as jnp
from jax import lax
from jax.experimental import pallas as pl
from jax.experimental.pallas import tpu as pltpu
from jax.sharding import PartitionSpec as P

F32, BF16, I32 = jnp.float32, jnp.bfloat16, jnp.int32
MESH = pl.DeviceIdType.MESH
LANES, SUBS = 128, 8
RATIO = 0.5
UNROLL = 2
VMEM_BYTES = 64 * 1024 * 1024 - 64 * 1024
ROWS = 8
NT = (((1,), (1,)), ((), ()))


def dot(a, b):
    return jnp.dot(a, b, preferred_element_type=F32)


def dot_nt(a, b):
    return lax.dot_general(a, b, NT, preferred_element_type=F32)


def split(value, parts):
    pieces = []
    for _ in range(parts):
        piece = value.astype(BF16).astype(F32)
        pieces.append(piece)
        value = value - piece
    return pieces


def wall_back(p, cond8):
    flux = cond8 * (pltpu.roll(p, ROWS - 1, 0) - p)
    return p + flux - pltpu.roll(flux, 1, 0)


def kernel(
    dims,
    kappa_ref,
    table_ref,
    wall_hbm,
    cond_hbm,
    face_hbm,
    owner_hbm,
    mat_hbm,
    air_hbm,
    speed_hbm,
    upwind_hbm,
    air_out,
    returned_out,
    ranks_out,
    wall_ref,
    cond_ref,
    face_ref,
    owner_ref,
    mat_ref,
    air_even,
    air_odd,
    speed,
    upwind,
    in_z,
    in_x,
    in_y,
    centre_c,
    out_x_last,
    in_x_last,
    in_z_halo,
    in_x_halo,
    halo_z,
    halo_x,
    edge_x,
    fix_x,
    field_t,
    row_hot,
    col_hot,
    flows_ref,
    added,
    parts_ref,
    rank_hot,
    ranks_ref,
    parcel,
    served,
    result,
    returned,
    load_sem,
    store_sem,
    in_send,
    in_recv,
    halo_send,
    halo_recv,
    parcel_send,
    parcel_recv,
    return_send,
    return_recv,
):
    steps, groups, columns = dims
    airs = (air_even, air_odd)
    fields, depth, breadth, span = air_out.shape
    walls = face_ref.shape[1]
    cap = rank_hot.shape[0]
    rows = depth * breadth
    x_tiles = breadth // SUBS
    chunks, _, chunk = served.shape
    per_chunk = chunk // cap
    me = lax.axis_index("vert")
    col = lax.axis_index("horiz")
    above, below = lax.rem(me + 1, groups), lax.rem(me + groups - 1, groups)
    east, west = lax.rem(col + 1, columns), lax.rem(col + columns - 1, columns)
    has_below = jnp.where(me > 0, 1.0, 0.0).astype(F32)
    has_above = jnp.where(me < groups - 1, 1.0, 0.0).astype(F32)
    has_west = jnp.where(col > 0, 1.0, 0.0).astype(F32)
    has_east = jnp.where(col < columns - 1, 1.0, 0.0).astype(F32)

    barrier = pltpu.get_barrier_semaphore()

    def greet(d, carry):
        pl.semaphore_signal(
            barrier, inc=1, device_id={"vert": lax.rem(me + d, groups)}, device_id_type=MESH
        )
        return carry

    loads = [
        pltpu.make_async_copy(src, dst, load_sem.at[k])
        for k, (src, dst) in enumerate(
            [
                (owner_hbm, owner_ref),
                (face_hbm, face_ref),
                (mat_hbm, mat_ref),
                (wall_hbm, wall_ref),
                (cond_hbm, cond_ref),
                (air_hbm, air_even.at[:, pl.ds(1, depth)]),
                (speed_hbm, speed),
                (upwind_hbm, upwind),
            ]
        )
    ]
    for load in loads:
        load.start()
    lax.fori_loop(1, groups, greet, 0)
    for neighbour in (east, west):
        pl.semaphore_signal(barrier, inc=1, device_id={"horiz": neighbour}, device_id_type=MESH)

    plane0 = jnp.zeros((fields, breadth, span), F32)
    for air in airs:
        air[:, 0] = plane0
        air[:, depth + 1] = plane0
    in_z[0] = jnp.zeros((breadth, span), F32)
    result[...] = jnp.zeros_like(result)

    loads[0].wait()
    owned = (lax.broadcasted_iota(I32, (groups, walls), 0) == owner_ref[...]).astype(F32)
    block = 2 * LANES
    blocks = walls // block
    stacked = jnp.concatenate(
        [owned[:, k * block : (k + 1) * block] for k in range(blocks)], axis=0
    )
    lower = (
        lax.broadcasted_iota(I32, (block, block), 0) < lax.broadcasted_iota(I32, (block, block), 1)
    ).astype(F32)
    before = dot(stacked.astype(BF16), lower.astype(BF16))
    totals = jnp.sum(stacked, axis=1, keepdims=True)
    offset = jnp.zeros((groups, 1), F32)
    ranks = []
    for k in range(blocks):
        part = slice(k * groups, (k + 1) * groups)
        ranks.append(
            jnp.sum(stacked[part] * (before[part] + offset), axis=0, keepdims=True)
        )
        offset = offset + totals[part]
    ranks = jnp.concatenate(ranks, axis=1).astype(I32)
    ranks_ref[...] = ranks
    rank_hot[...] = (
        (lax.broadcasted_iota(I32, (cap, walls), 0) == ranks).astype(F32).astype(BF16)
    )

    for load in loads[1:5]:
        load.wait()
    material = mat_ref[...]
    hcoef = jnp.zeros(material.shape, F32)
    for k in range(table_ref.shape[0]):
        hcoef = jnp.where(material == k, table_ref[k], hcoef)
    layer = lax.broadcasted_iota(I32, (ROWS, walls), 0)
    surface = (layer == 0).astype(F32)
    cond8 = jnp.concatenate([cond_ref[...], jnp.zeros((1, walls), F32)], axis=0)
    h_top = surface * hcoef
    p = wall_ref[...]
    e = surface
    values = [face_ref[...].astype(F32), hcoef]
    for step in range(steps):
        values.append(p[0:1])
        if step < steps - 1:
            p = wall_back(p, cond8) - h_top * p
    for _ in range(steps - 2):
        e = wall_back(e, cond8) - h_top * e
        values.append(e[0:1])
    values = jnp.concatenate(values, axis=0)
    for s, piece in enumerate(split(values, 3)):
        for b in range(0, groups, 2):
            pair = jnp.concatenate([piece * owned[b : b + 1], piece * owned[b + 1 : b + 2]], axis=0)
            parts_ref[pl.ds((s * groups + b) * ROWS, 2 * ROWS), :] = pair.astype(BF16)
    placed = dot_nt(parts_ref[...], rank_hot[...])
    n = groups * ROWS
    parcel[...] = placed[:n] + placed[n : 2 * n] + placed[2 * n :]

    def at_rows(k):
        return pl.ds(pl.multiple_of(k * ROWS, ROWS), ROWS)

    def at_lanes(k):
        return pl.ds(pl.multiple_of(lax.rem(k, per_chunk) * cap, cap), cap)

    served[lax.div(me, per_chunk), :, at_lanes(me)] = parcel[at_rows(me), :]

    pl.semaphore_wait(barrier, groups + 1)

    def parcel_copy(d):
        to = lax.rem(me + d, groups)
        return pltpu.make_async_remote_copy(
            src_ref=parcel.at[at_rows(to)],
            dst_ref=served.at[lax.div(me, per_chunk), :, at_lanes(me)],
            send_sem=parcel_send.at[d],
            recv_sem=parcel_recv.at[d],
            device_id={"vert": to},
            device_id_type=MESH,
        )

    def return_copy(d):
        to = lax.rem(me + d, groups)
        return pltpu.make_async_remote_copy(
            src_ref=result.at[lax.div(to, per_chunk), :, at_lanes(to)],
            dst_ref=returned.at[at_rows(me)],
            send_sem=return_send.at[d],
            recv_sem=return_recv.at[d],
            device_id={"vert": to},
            device_id_type=MESH,
        )

    def each(copy, act):
        def body(d, carry):
            act(copy(d))
            return carry

        lax.fori_loop(1, groups, body, 0)

    each(parcel_copy, lambda copy: copy.start())

    def halo_copies(step, air, first, count, group):
        some = pl.ds(first, count)
        return [
            pltpu.make_async_remote_copy(
                src_ref=src,
                dst_ref=dst,
                send_sem=halo_send.at[step, group, k],
                recv_sem=halo_recv.at[step, group, k],
                device_id=to,
                device_id_type=MESH,
            )
            for k, (src, dst, to) in enumerate(
                [
                    (air.at[some, depth], halo_z.at[step, 0, some], {"vert": above}),
                    (air.at[some, 1], halo_z.at[step, 1, some], {"vert": below}),
                    (edge_x.at[step, 1, some], halo_x.at[step, 0, some], {"horiz": east}),
                    (edge_x.at[step, 0, some], halo_x.at[step, 1, some], {"horiz": west}),
                ]
            )
        ]

    pairs = halo_recv.shape[1] - 1
    paired = (fields - 1) // pairs

    def halos_of(step, air, group):
        if isinstance(group, int) and group == pairs:
            return halo_copies(step, air, 0, 1, pairs)
        return halo_copies(step, air, 1 + group * paired, paired, group)

    planes = LANES // breadth

    def split_field(air):
        def body(k, carry):
            block = air[0, pl.ds(1 + k * planes, planes)].reshape(LANES, span).T
            hi = block.astype(BF16)
            field_t[:, pl.ds(pl.multiple_of(k * LANES, LANES), LANES)] = hi
            field_t[:, pl.ds(pl.multiple_of(rows + k * LANES, LANES), LANES)] = (
                block - hi.astype(F32)
            ).astype(BF16)
            return carry

        for k in range(depth // planes):
            body(k, 0)

    loads[5].wait()

    def pack_first(z, carry):
        for f in range(fields):
            edge_x[0, 0, f, pl.ds(z, 1), :] = air_even[f, z + 1, 0:1, :]
            edge_x[0, 1, f, pl.ds(z, 1), :] = air_even[f, z + 1, breadth - 1 : breadth, :]
        return carry

    lax.fori_loop(0, depth, pack_first, 0)
    for group in range(pairs + 1):
        for copy in halos_of(0, air_even, group):
            copy.start()
    split_field(air_even)

    loads[6].wait()
    loads[7].wait()
    row_id = lax.broadcasted_iota(I32, (breadth, span), 0)
    lane_id = lax.broadcasted_iota(I32, (breadth, span), 1)

    def coefficients(z, carry):
        out, inn = [], []
        for d in range(3):
            s = speed[d, z]
            o = s * upwind[d, z].astype(F32)
            out.append(o)
            inn.append(s - o)
            speed[d, z] = o
        in_z[z + 1] = -inn[0]
        in_x_last[pl.ds(z, 1), :] = -inn[1][breadth - 1 : breadth]
        out_x_last[pl.ds(z, 1), :] = out[1][breadth - 1 : breadth]
        low_x = jnp.where(row_id == 0, 0.0, pltpu.roll(-inn[1], 1, 0))
        low_y = jnp.where(lane_id == 0, 0.0, pltpu.roll(-inn[2], 1, 1))
        in_x[z] = low_x
        in_y[z] = low_y
        centre_c[z] = 1.0 - (out[0] + out[1] + out[2]) - (in_z[z] + low_x + low_y)
        return carry

    lax.fori_loop(0, depth, coefficients, 0)
    in_copies = [
        pltpu.make_async_remote_copy(
            src_ref=src,
            dst_ref=dst,
            send_sem=in_send.at[k],
            recv_sem=in_recv.at[k],
            device_id=to,
            device_id_type=MESH,
        )
        for k, (src, dst, to) in enumerate(
            [
                (in_z.at[depth], in_z_halo, {"vert": above}),
                (in_x_last, in_x_halo, {"horiz": east}),
            ]
        )
    ]
    for copy in in_copies:
        copy.start()

    sub8 = lax.broadcasted_iota(I32, (SUBS, LANES), 0)
    lane8 = lax.broadcasted_iota(I32, (SUBS, LANES), 1)

    def stencil(cur, new, z, chosen):
        zero = jnp.zeros((SUBS, LANES), F32)
        first_lane, last_lane = lane8 == 0, lane8 == LANES - 1
        first_sub, last_sub = sub8 == 0, sub8 == SUBS - 1
        for f in chosen:
            kappa = kappa_ref[f]
            tile = {}
            for i in range(x_tiles):
                for h in range(2):
                    tile[i, h] = cur[
                        f, z + 1, SUBS * i : SUBS * (i + 1), LANES * h : LANES * (h + 1)
                    ]
            down = {k: pltpu.roll(t, 1, 0) for k, t in tile.items()}
            up = {k: pltpu.roll(t, SUBS - 1, 0) for k, t in tile.items()}
            for i in range(x_tiles):
                right = [pltpu.roll(tile[i, h], 1, 1) for h in range(2)]
                left = [pltpu.roll(tile[i, h], LANES - 1, 1) for h in range(2)]
                south = [jnp.where(first_lane, 0.0, right[0]), jnp.where(first_lane, *right)]
                north = [
                    jnp.where(last_lane, left[1], left[0]),
                    jnp.where(last_lane, 0.0, left[1]),
                ]
                for h in range(2):
                    at = (slice(SUBS * i, SUBS * (i + 1)), slice(LANES * h, LANES * (h + 1)))
                    m_west = jnp.where(first_sub, down[i - 1, h] if i else zero, down[i, h])
                    m_east = jnp.where(
                        last_sub, up[i + 1, h] if i + 1 < x_tiles else zero, up[i, h]
                    )
                    total = (centre_c[(z,) + at] - 6.0 * kappa) * tile[i, h]
                    total += (speed[(0, z) + at] + kappa) * cur[(f, z + 2) + at]
                    total += (in_z[(z,) + at] + kappa) * cur[(f, z) + at]
                    total += (speed[(1, z) + at] + kappa) * m_east
                    total += (in_x[(z,) + at] + kappa) * m_west
                    total += (speed[(2, z) + at] + kappa) * north[h]
                    total += (in_y[(z,) + at] + kappa) * south[h]
                    new[(f, z + 1) + at] = total

    def stencil_first(z, carry):
        stencil(air_even, air_odd, z, range(fields))
        return carry

    lax.fori_loop(0, depth, stencil_first, 0)
    each(parcel_copy, lambda copy: copy.wait())

    def one_hots(c, carry):
        cell = served[c, 0:1, :].astype(I32)
        hot = (lax.broadcasted_iota(I32, (rows, chunk), 0) == cell // span).astype(F32).astype(BF16)
        row_hot[c, :rows] = hot
        row_hot[c, rows:] = hot
        col_hot[c] = (
            (lax.broadcasted_iota(I32, (span, chunk), 0) == cell % span).astype(F32).astype(BF16)
        )
        return carry

    lax.fori_loop(0, chunks, one_hots, 0)

    def gather(step, c):
        picked = dot(field_t[...], row_hot[c])
        wall = served[c]
        y = wall[0:1].astype(I32) % span
        mask = lax.broadcasted_iota(I32, (span, chunk), 0) == y
        fetched = jnp.sum(jnp.where(mask, picked, 0.0), axis=0, keepdims=True)
        h = wall[1:2]
        half = RATIO * fetched * h
        flow = h * wall[2:3] - half
        flows_ref[pl.ds(c, 1), :] = flow
        result[c, pl.ds(step, 1), :] = flow
        later = [wall[0:1], h, wall[3:4] + half]
        for k in range(1, steps - 1):
            g = steps + 1 + k
            later.append(wall[3 + k : 4 + k] + half * wall[g : g + 1])
        later.append(jnp.zeros_like(h))
        later.append(wall[2 + steps :])
        served[c] = jnp.concatenate(later, axis=0)

    def scatter(c):
        flow = flows_ref[pl.ds(c, 1), :]
        hi = flow.astype(BF16)
        lo = (flow - hi.astype(F32)).astype(BF16)
        hot = col_hot[c]
        where = row_hot[c, :rows]
        added[...] += dot_nt(where, hot * hi) + dot_nt(where, hot * lo)

    def beyond_z(step, cur, new, f):
        kappa = kappa_ref[f]
        beyond = halo_z[step, 0, f] * has_below
        new[f, 1] += kappa * beyond + in_z_halo[...] * (beyond - cur[f, 1])
        beyond = halo_z[step, 1, f] * has_above
        new[f, depth] += (speed[0, depth - 1] + kappa) * beyond
        beyond = halo_x[step, 0, f] * has_west
        fix_x[0, f] = kappa * beyond + in_x_halo[...] * (beyond - edge_x[step, 0, f])
        beyond = halo_x[step, 1, f] * has_east
        fix_x[1, f] = (out_x_last[...] + kappa) * beyond

    def finish(step, cur, new, chosen, walls_too=False):
        for f in chosen:
            beyond_z(step, cur, new, f)

        def body(k, carry):
            for j in range(UNROLL):
                z = k * UNROLL + j
                if walls_too:
                    at = pl.ds(pl.multiple_of(z * breadth, breadth), breadth)
                    new[0, z + 1] += added[at, :]
                for f in chosen:
                    low = new[f, z + 1, 0:1, :] + fix_x[0, f, pl.ds(z, 1), :]
                    high = (
                        new[f, z + 1, breadth - 1 : breadth, :] + fix_x[1, f, pl.ds(z, 1), :]
                    )
                    new[f, z + 1, 0:1, :] = low
                    new[f, z + 1, breadth - 1 : breadth, :] = high
                    edge_x[step + 1, 0, f, pl.ds(z, 1), :] = low
                    edge_x[step + 1, 1, f, pl.ds(z, 1), :] = high
            return carry

        lax.fori_loop(0, depth // UNROLL, body, 0)

    def store(f):
        return pltpu.make_async_copy(
            airs[steps % 2].at[f, pl.ds(1, depth)], air_out.at[f], store_sem.at[f]
        )

    rank_store = pltpu.make_async_copy(ranks_ref, ranks_out, store_sem.at[fields])
    rank_store.start()
    returned_store = pltpu.make_async_copy(returned, returned_out, store_sem.at[fields + 1])

    beside = depth // chunks

    def time_step(step, cur, new):
        last = step == steps - 1
        even = cur is air_even

        def never(act):
            return None

        def always(act):
            act()

        when_first = pl.when(step == 0) if even else never
        unless_first = pl.when(step > 0) if even else always
        when_last = never if even else pl.when(last)
        unless_last = always if even else pl.when(jnp.logical_not(last))

        def body_gather(c, carry):
            @when_first
            def _():
                gather(step, c)

            @unless_first
            def _():
                gather(step, c)
                for k in range(beside):
                    stencil(cur, new, c * beside + k, range(1, 1 + paired))

            @when_last
            def _():
                def send_back(k, carry):
                    d = lax.rem(c * per_chunk + k - me + groups, groups)

                    @pl.when(d > 0)
                    def _():
                        return_copy(d).start()

                    return carry

                lax.fori_loop(0, per_chunk, send_back, 0)

            return carry

        lax.fori_loop(0, chunks, body_gather, 0)

        @when_last
        def _():
            returned[at_rows(me), :] = result[lax.div(me, per_chunk), :, at_lanes(me)]

        @when_first
        def _():
            for copy in in_copies:
                copy.wait()
            in_z_halo[...] = in_z_halo[...] * has_below
            in_x_halo[...] = in_x_halo[...] * has_west

        def apply_halos(group):
            chosen = [1 + group * paired + k for k in range(paired)]
            for copy in halos_of(step, cur, group):
                copy.wait()
            finish(step, cur, new, chosen)

            @when_last
            def _():
                for f in chosen:
                    store(f).start()

            @unless_last
            def _():
                for copy in halos_of(step + 1, new, group):
                    copy.start()

        apply_halos(0)
        added[...] = jnp.zeros_like(added)

        def body_scatter(c, carry):
            @when_first
            def _():
                scatter(c)

            @unless_first
            def _():
                scatter(c)
                for k in range(beside):
                    stencil(cur, new, c * beside + k, [0, *range(1 + paired, fields)])

            return carry

        lax.fori_loop(0, chunks, body_scatter, 0)
        for group in range(1, pairs):
            apply_halos(group)
        for copy in halos_of(step, cur, pairs):
            copy.wait()
        finish(step, cur, new, range(1), True)

        @when_last
        def _():
            store(0).start()

        @unless_last
        def _():
            for copy in halos_of(step + 1, new, pairs):
                copy.start()
            split_field(new)

    def two_steps(k, carry):
        time_step(2 * k, air_even, air_odd)
        time_step(2 * k + 1, air_odd, air_even)
        return carry

    lax.fori_loop(0, steps // 2, two_steps, 0)
    each(return_copy, lambda copy: copy.wait())
    returned_store.start()
    for copy in [rank_store, returned_store] + [store(f) for f in range(fields)]:
        copy.wait()


def wall_kernel(
    dims,
    air_hbm,
    returned_hbm,
    ranks_hbm,
    owner_hbm,
    wall_hbm,
    cond_hbm,
    saved_hbm,
    air_out,
    wall_out,
    grad_out,
    air,
    returned,
    ranks_ref,
    owner_ref,
    wall_ref,
    cond_ref,
    saved_ref,
    wall_res,
    grad_res,
    load_sem,
    store_sem,
):
    steps, groups = dims
    fields = air.shape[0]
    cap = returned.shape[1]
    walls = wall_ref.shape[1]
    loads = [
        pltpu.make_async_copy(src, dst, load_sem.at[k])
        for k, (src, dst) in enumerate(
            [(air_hbm.at[f], air.at[f]) for f in range(fields)]
            + [
                (ranks_hbm, ranks_ref),
                (owner_hbm, owner_ref),
                (returned_hbm, returned),
                (wall_hbm, wall_ref),
                (cond_hbm, cond_ref),
                (saved_hbm, saved_ref),
            ]
        )
    ]
    for load in loads:
        load.start()
    stores = [
        pltpu.make_async_copy(air.at[f], air_out.at[f], store_sem.at[f]) for f in range(fields)
    ] + [
        pltpu.make_async_copy(wall_res, wall_out, store_sem.at[fields]),
        pltpu.make_async_copy(grad_res, grad_out, store_sem.at[fields + 1]),
    ]
    for f in range(fields):
        loads[f].wait()
        stores[f].start()
    for load in loads[fields:]:
        load.wait()
    rank_hot = (
        (lax.broadcasted_iota(I32, (cap, walls), 0) == ranks_ref[...]).astype(F32).astype(BF16)
    )
    owned = (lax.broadcasted_iota(I32, (groups, walls), 0) == owner_ref[...]).astype(F32)
    placed = dot(jnp.concatenate(split(returned[...], 3), axis=0).astype(BF16), rank_hot)
    n = groups * ROWS
    placed = placed[:n] + placed[n : 2 * n] + placed[2 * n :]
    flows = jnp.zeros((ROWS, walls), F32)
    for b in range(groups):
        flows = flows + owned[b : b + 1] * placed[b * ROWS : (b + 1) * ROWS]
    surface = (lax.broadcasted_iota(I32, (ROWS, walls), 0) == 0).astype(F32)
    p = wall_ref[...]
    cond8 = jnp.concatenate([cond_ref[...], jnp.zeros((1, walls), F32)], axis=0)
    grad = jnp.zeros((ROWS, walls), F32)
    for step in range(steps):
        saved = saved_ref[steps - 1 - step]
        grad = grad - (pltpu.roll(saved, ROWS - 1, 0) - saved) * (pltpu.roll(p, ROWS - 1, 0) - p)
        p = wall_back(p, cond8) - surface * flows[step : step + 1]
    wall_res[...] = p
    grad_res[...] = grad[: ROWS - 1]
    for copy in stores[fields:]:
        copy.start()
    for copy in stores:
        copy.wait()


def per_device(
    air_seed,
    wall_seed,
    speed,
    upwind,
    diffusivity,
    conductivity,
    wall_saved,
    heat_table,
    interface,
    owner,
    material,
):
    groups, columns = lax.axis_size("vert"), lax.axis_size("horiz")
    steps = wall_saved.shape[0]
    walls = interface.shape[0]
    cap = walls // 4
    fields, depth, breadth, span = air_seed.shape
    rows = depth * breadth
    chunks = 2
    pairs = 2
    chunk = groups * cap // chunks
    smem = pl.BlockSpec(memory_space=pltpu.SMEM)
    hbm = pl.BlockSpec(memory_space=pl.ANY)
    dma = pltpu.SemaphoreType.DMA
    plane = (breadth, span)
    brick = (depth, breadth, span)
    side = (depth, span)
    scratch = [
        pltpu.VMEM(wall_seed.shape, F32),
        pltpu.VMEM(conductivity.shape, F32),
        pltpu.VMEM((1, walls), I32),
        pltpu.VMEM((1, walls), I32),
        pltpu.VMEM((1, walls), I32),
        pltpu.VMEM((fields, depth + 2) + plane, F32),
        pltpu.VMEM((fields, depth + 2) + plane, F32),
        pltpu.VMEM((3,) + brick, F32),
        pltpu.VMEM((3,) + brick, I32),
        pltpu.VMEM((depth + 1,) + plane, F32),
        pltpu.VMEM(brick, F32),
        pltpu.VMEM(brick, F32),
        pltpu.VMEM(brick, F32),
        pltpu.VMEM(side, F32),
        pltpu.VMEM(side, F32),
        pltpu.VMEM(plane, F32),
        pltpu.VMEM(side, F32),
        pltpu.VMEM((steps, 2, fields) + plane, F32),
        pltpu.VMEM((steps, 2, fields) + side, F32),
        pltpu.VMEM((steps + 1, 2, fields) + side, F32),
        pltpu.VMEM((2, fields) + side, F32),
        pltpu.VMEM((span, 2 * rows), BF16),
        pltpu.VMEM((chunks, 2 * rows, chunk), BF16),
        pltpu.VMEM((chunks, span, chunk), BF16),
        pltpu.VMEM((chunks, chunk), F32),
        pltpu.VMEM((rows, span), F32),
        pltpu.VMEM((3 * groups * ROWS, walls), BF16),
        pltpu.VMEM((cap, walls), BF16),
        pltpu.VMEM((1, walls), I32),
        pltpu.VMEM((groups * ROWS, cap), F32),
        pltpu.VMEM((chunks, ROWS, chunk), F32),
        pltpu.VMEM((chunks, ROWS, chunk), F32),
        pltpu.VMEM((groups * ROWS, cap), F32),
        dma((8,)),
        dma((fields + 2,)),
        dma((2,)),
        dma((2,)),
        dma((steps, pairs + 1, 4)),
        dma((steps, pairs + 1, 4)),
        dma((groups,)),
        dma((groups,)),
        dma((groups,)),
        dma((groups,)),
    ]
    owners = owner.reshape(1, walls)
    air, returned, ranks = pl.pallas_call(
        functools.partial(kernel, (steps, groups, columns)),
        out_shape=(
            jax.ShapeDtypeStruct(air_seed.shape, F32),
            jax.ShapeDtypeStruct((groups * ROWS, cap), F32),
            jax.ShapeDtypeStruct((1, walls), I32),
        ),
        in_specs=[smem, smem] + [hbm] * 8,
        out_specs=(hbm, hbm, hbm),
        scratch_shapes=scratch,
        compiler_params=pltpu.CompilerParams(
            collective_id=0, has_side_effects=True, vmem_limit_bytes=VMEM_BYTES
        ),
        cost_estimate=pl.CostEstimate(
            flops=2 * steps * 4 * groups * cap * rows * span,
            bytes_accessed=40 * rows * span,
            transcendentals=0,
        ),
    )(
        diffusivity,
        heat_table,
        wall_seed,
        conductivity,
        interface.reshape(1, walls),
        owners,
        material.reshape(1, walls),
        air_seed,
        speed,
        upwind,
    )
    return pl.pallas_call(
        functools.partial(wall_kernel, (steps, groups)),
        out_shape=(
            jax.ShapeDtypeStruct(air_seed.shape, F32),
            jax.ShapeDtypeStruct(wall_seed.shape, F32),
            jax.ShapeDtypeStruct(conductivity.shape, F32),
        ),
        in_specs=[hbm] * 7,
        out_specs=(hbm, hbm, hbm),
        scratch_shapes=[
            pltpu.VMEM(air_seed.shape, F32),
            pltpu.VMEM((groups * ROWS, cap), F32),
            pltpu.VMEM((1, walls), I32),
            pltpu.VMEM((1, walls), I32),
            pltpu.VMEM(wall_seed.shape, F32),
            pltpu.VMEM(conductivity.shape, F32),
            pltpu.VMEM(wall_saved.shape, F32),
            pltpu.VMEM(wall_seed.shape, F32),
            pltpu.VMEM(conductivity.shape, F32),
            dma((6 + fields,)),
            dma((2 + fields,)),
        ],
        compiler_params=pltpu.CompilerParams(vmem_limit_bytes=VMEM_BYTES),
        cost_estimate=pl.CostEstimate(
            flops=2 * 3 * groups * ROWS * cap * walls,
            bytes_accessed=48 * rows * span,
            transcendentals=0,
        ),
    )(air, returned, ranks, owners, wall_seed, conductivity, wall_saved)


def solution(mesh):
    air = P(None, "vert", "horiz", None)
    wall = P(None, ("horiz", "vert"))
    column = P(("horiz", "vert"))
    return jax.shard_map(
        per_device,
        mesh=mesh,
        in_specs=(
            air,
            wall,
            air,
            air,
            P(),
            wall,
            P(None, None, ("horiz", "vert")),
            P(),
            column,
            P(("horiz", "vert"), None),
            column,
        ),
        out_specs=(air, wall, wall),
        check_vma=False,
    )
```
